128 devices in a mesh: row: 8 (over x, z_lo), col: 16 (over z_hi, y, core).
Axes of the slice: x: 4, y: 4, z: 4 (z_hi: 2, z_lo: 2; z = z_hi * 2 + z_lo), core: 2. Of those that a mesh axis runs over, the one named last changes fastest.
Arguments:
- features: bfloat16 [65536, 256], P(('row', 'col')), may hold values from -6 to 6
- weight: bfloat16 [256, 256], replicated, may hold values from -0.375 to 0.375
- tile_values: bfloat16 [8, 16, 192, 128, 128], P('row', 'col'), may hold values from -0.078125 to 0.078125
- tile_coords: int32 [8, 16, 192, 2], P('row', 'col'), may hold values from 0 to 63, as said below
- tile_counts: int32 [8, 16], P('row', 'col'), may hold values from 48 to 192, as said below
- out_grad: bfloat16 [65536, 256], P(('row', 'col')), may hold values from -6 to 6
Outputs:
- activated: bfloat16 [65536, 256], P(('row', 'col'))
- weight_grad: float32 [256, 256], replicated
- feature_grad: bfloat16 [65536, 256], P(('row', 'col'))
The draws below stay inside these ranges and needn't reach their ends.
Inputs may be any that keep to these rules, and one draw needn't show every extreme that they name: `tile_coords`: within one block the slots name distinct tiles; tile rows are below 64 and tile columns below 32. `tile_counts`: slots at or past a block's count are not part of the adjacency. Some block has 192 live slots.
All inputs are finite; a program needn't handle non-finite values.
Results may differ from the reference program's by a relative error of at most 0.006.
Values may be sent and summed in bfloat16 or wider, within the bound.
A program may use at most 192 MiB of HBM per device.

```python
import jax
import jax.numpy as jnp
from jax import lax

FEAT = 256
TILE = 128
NODES_DEV = 512
TILES_DEV = 192
NODES = 65536
ROW_TILES = 64
COL_TILES = 32
N_ROW = 8
N_COL = 16


def draw_tile_coords(key, part):
    key = jax.random.fold_in(key, 11)
    block_keys = jax.random.split(key, N_ROW * N_COL)

    def one_block(block_key):
        chosen = jax.random.permutation(block_key, ROW_TILES * COL_TILES)[:TILES_DEV]
        return jnp.stack([chosen // COL_TILES, chosen % COL_TILES], axis=-1).astype(jnp.int32)
    return jax.vmap(one_block)(block_keys).reshape(N_ROW, N_COL, TILES_DEV, 2)


def draw_tile_counts(key, part):
    key = jax.random.fold_in(key, 23)
    first_key, second_key = jax.random.split(key)
    counts = jax.random.randint(first_key, (N_ROW * N_COL,), TILES_DEV // 4, TILES_DEV + 1).astype(jnp.int32)
    busiest = jax.random.randint(second_key, (), 0, N_ROW * N_COL)
    counts = counts.at[busiest].set(TILES_DEV)
    return counts.reshape(N_ROW, N_COL).astype(jnp.int32)


def block_scale(key, shape, cuts, low, high):
    gain = 1.0
    for axis_at, shards_of in cuts:
        heights = jax.random.uniform(jax.random.fold_in(jax.random.fold_in(key, 6), axis_at), (shards_of,), jnp.float32, low / len(cuts), high / len(cuts))
        gain = gain * jnp.repeat(jnp.exp(heights), shape[axis_at] // shards_of).reshape((-1,) + (1,) * (len(shape) - 1 - axis_at))
    return gain


def centred(key, dims, spread, most, cuts=(), kind=jnp.bfloat16):
    entries = spread * jax.random.normal(key, dims, jnp.float32)
    if cuts:
        entries = entries * block_scale(key, dims, cuts, -0.22, 0.18)
    return jnp.clip(entries, -most, most).astype(kind)


def setup_inputs(seed: int = 0) -> dict:
    splits = jax.random.split(jax.random.key(seed), 7)
    return {
        "features": centred(splits[0], (NODES, FEAT), 1.0, 6.0, ((0, 128),)),
        "weight": centred(splits[1], (FEAT, FEAT), FEAT ** -0.5, 0.375),
        "tile_values": centred(splits[2], (N_ROW, N_COL, TILES_DEV, TILE, TILE), (TILE * TILE * TILES_DEV // NODES_DEV) ** -0.5, 0.078125, ((0, 8), (1, 16))),
        "tile_coords": draw_tile_coords(jax.random.fold_in(splits[6], 71), 0),
        "tile_counts": draw_tile_counts(jax.random.fold_in(splits[6], 71), 0),
        "out_grad": centred(splits[5], (NODES, FEAT), 1.0, 6.0, ((0, 128),)),
    }


def silu_grad(value):
    sigma = jax.nn.sigmoid(value)
    return sigma * (1.0 + value * (1.0 - sigma))

def reference(features, weight, tile_values, tile_coords, tile_counts, out_grad):
    groups = features.reshape(N_ROW, N_COL, NODES_DEV, FEAT)
    slot_ids = jnp.arange(TILES_DEV, dtype=jnp.int32)

    def forward_row(row_index):

        def over_col(carried, col_index):
            source = lax.dynamic_index_in_dim(groups, col_index, 1, keepdims=False)
            source = source.reshape(COL_TILES, TILE, FEAT)
            tile_set = tile_values[row_index, col_index]
            coords = tile_coords[row_index, col_index]
            count = tile_counts[row_index, col_index]
            picked = source[coords[:, 1]]
            product = jnp.einsum('kij,kjf->kif', tile_set.astype(jnp.float32), picked.astype(jnp.float32))
            segment_ids = jnp.where(slot_ids < count, coords[:, 0], ROW_TILES).astype(jnp.int32)
            return (carried + jax.ops.segment_sum(product, segment_ids, num_segments=ROW_TILES), None)
        start = jnp.zeros((ROW_TILES, TILE, FEAT), jnp.float32)
        summed, unused = lax.scan(over_col, start, jnp.arange(N_COL, dtype=jnp.int32))
        return summed.reshape(N_COL * NODES_DEV, FEAT)
    aggregated = lax.map(forward_row, jnp.arange(N_ROW, dtype=jnp.int32)).reshape(NODES, FEAT).astype(jnp.bfloat16)
    pre = jnp.dot(aggregated, weight, preferred_element_type=jnp.float32)
    activated = jax.nn.silu(pre).astype(jnp.bfloat16)
    pre_grad = (out_grad.astype(jnp.float32) * silu_grad(pre)).astype(jnp.bfloat16)
    weight_grad = jnp.dot(aggregated.T, pre_grad, preferred_element_type=jnp.float32) * NODES ** (-0.5)
    agg_grad = jnp.dot(pre_grad, weight.T, preferred_element_type=jnp.float32).astype(jnp.bfloat16)
    grad_blocks = agg_grad.reshape(N_ROW, N_COL * NODES_DEV, FEAT)

    def backward_col(col_index):

        def over_row(carried, row_index):
            source = lax.dynamic_index_in_dim(grad_blocks, row_index, 0, keepdims=False)
            source = source.reshape(ROW_TILES, TILE, FEAT)
            tile_set = tile_values[row_index, col_index]
            coords = tile_coords[row_index, col_index]
            count = tile_counts[row_index, col_index]
            picked = source[coords[:, 0]]
            product = jnp.einsum('kij,kif->kjf', tile_set.astype(jnp.float32), picked.astype(jnp.float32))
            segment_ids = jnp.where(slot_ids < count, coords[:, 1], COL_TILES).astype(jnp.int32)
            return (carried + jax.ops.segment_sum(product, segment_ids, num_segments=COL_TILES), None)
        start = jnp.zeros((COL_TILES, TILE, FEAT), jnp.float32)
        summed, unused = lax.scan(over_row, start, jnp.arange(N_ROW, dtype=jnp.int32))
        return summed.reshape(N_ROW, NODES_DEV, FEAT)
    pieces = lax.map(backward_col, jnp.arange(N_COL, dtype=jnp.int32))
    feature_grad = jnp.transpose(pieces, (1, 0, 2, 3)).reshape(NODES, FEAT).astype(jnp.bfloat16)
    return (activated, weight_grad, feature_grad)
```

```python
import functools

import jax
import jax.numpy as jnp
from jax import lax
from jax.experimental import pallas as pl
from jax.experimental.pallas import tpu as pltpu
from jax.sharding import PartitionSpec as P

MESH = pl.DeviceIdType.MESH
TILE = 128
SLOTS = 192
ROW_TILES = 64
COL_TILES = 32
OWN = 4
HALF = 2
PREV_F, SRC_F, LAST_F = 0, SLOTS, 2 * SLOTS
PREV_B = 2 * SLOTS + ROW_TILES
SRC_B, LAST_B = PREV_B + SLOTS, PREV_B + 2 * SLOTS
R_FARP, R_NEARP_U, R_NEARP_D, R_FAR_U, R_FAR_D, R_NEAR_U, R_NEAR_D, R_PAIR = 0, 4, 8, 12, 14, 16, 20, 24
R_TILES = 28
F32 = jnp.float32
BF16 = jnp.bfloat16


def send(src, dst, ssem, rsem, device):
    copy = pltpu.make_async_remote_copy(
        src_ref=src, dst_ref=dst, send_sem=ssem, recv_sem=rsem, device_id=device, device_id_type=MESH
    )
    copy.start()
    return copy


def arrive(dst, ssem, rsem, device):
    pltpu.make_async_remote_copy(
        src_ref=dst, dst_ref=dst, send_sem=ssem, recv_sem=rsem, device_id=device, device_id_type=MESH
    ).wait_recv()


class Ring:
    def __init__(self, i, p, device, block):
        self.up, self.down, self.far = lax.rem(i + 1, 4), lax.rem(i + 3, 4), lax.rem(i + 2, 4)
        self.i, self.p, self.q = i, p, 1 - p
        self.d_up, self.d_down, self.d_pair = device(self.up, p), device(self.down, p), device(i, self.q)
        self.block = block


def gather(ring, buf, ss, rs, sent, landed=lambda name: None):
    i, p, q, up, down, far = ring.i, ring.p, ring.q, ring.up, ring.down, ring.far

    def part(i, p, first=0, count=OWN):
        return buf.at[pl.ds(ring.block(i, p) * OWN + first, count)]

    def go(n, what, device):
        sent.append(send(what, what, ss.at[n], rs.at[n], device))

    def got(n, what, device):
        arrive(what, ss.at[n], rs.at[n], device)

    go(0, part(i, p), ring.d_up)
    go(1, part(i, p), ring.d_down)
    go(2, part(i, p), ring.d_pair)
    landed((i, p))
    yield
    got(0, part(down, p), ring.d_down)
    go(3, part(down, p, 0, HALF), ring.d_up)
    got(1, part(up, p), ring.d_up)
    go(4, part(up, p, HALF, HALF), ring.d_down)
    got(2, part(i, q), ring.d_pair)
    go(5, part(i, q), ring.d_up)
    go(6, part(i, q), ring.d_down)
    landed((down, p))
    landed((up, p))
    landed((i, q))
    yield
    got(3, part(far, p, 0, HALF), ring.d_down)
    go(7, part(far, p, 0, HALF), ring.d_pair)
    got(4, part(far, p, HALF, HALF), ring.d_up)
    go(8, part(far, p, HALF, HALF), ring.d_pair)
    landed((far, p))
    yield
    got(5, part(down, q), ring.d_down)
    got(6, part(up, q), ring.d_up)
    landed((down, q))
    landed((up, q))
    got(7, part(far, q, 0, HALF), ring.d_pair)
    got(8, part(far, q, HALF, HALF), ring.d_pair)
    landed((far, q))
    yield


def reduce(ring, partial, out, sbuf, rbuf, ss, rs, sent):
    i, p, q, up, down, far = ring.i, ring.p, ring.q, ring.up, ring.down, ring.far

    def go(n, first, count, device):
        sent.append(
            send(sbuf.at[pl.ds(first, count)], rbuf.at[pl.ds(first, count)], ss.at[n], rs.at[n], device)
        )

    def got(n, first, count, device):
        arrive(rbuf.at[pl.ds(first, count)], ss.at[n], rs.at[n], device)

    def put(first, block, tiles=range(OWN), terms=()):
        for n, t in enumerate(tiles):
            total = partial(*block, t)
            for term in terms:
                total = total + rbuf[term + n].astype(F32)
            sbuf[first + n] = total.astype(BF16)

    put(R_FARP, (far, q))
    go(0, R_FARP, HALF, ring.d_pair)
    go(1, R_FARP + HALF, HALF, ring.d_pair)
    put(R_NEARP_U, (up, q))
    go(2, R_NEARP_U, OWN, ring.d_up)
    put(R_NEARP_D, (down, q))
    go(3, R_NEARP_D, OWN, ring.d_down)
    yield
    got(0, R_FARP, HALF, ring.d_pair)
    put(R_FAR_U, (far, p), (0, 1), (R_FARP,))
    go(4, R_FAR_U, HALF, ring.d_up)
    got(1, R_FARP + HALF, HALF, ring.d_pair)
    put(R_FAR_D, (far, p), (2, 3), (R_FARP + HALF,))
    go(5, R_FAR_D, HALF, ring.d_down)
    yield
    got(2, R_NEARP_U, OWN, ring.d_down)
    got(3, R_NEARP_D, OWN, ring.d_up)
    put(R_PAIR, (i, q), range(OWN), (R_NEARP_U, R_NEARP_D))
    go(6, R_PAIR, OWN, ring.d_pair)
    yield
    got(4, R_FAR_U, HALF, ring.d_down)
    put(R_NEAR_U, (up, p), (0, 1), (R_FAR_U,))
    put(R_NEAR_U + HALF, (up, p), (2, 3))
    go(7, R_NEAR_U, OWN, ring.d_up)
    got(5, R_FAR_D, HALF, ring.d_up)
    put(R_NEAR_D, (down, p), (0, 1))
    put(R_NEAR_D + HALF, (down, p), (2, 3), (R_FAR_D,))
    go(8, R_NEAR_D, OWN, ring.d_down)
    yield
    got(6, R_PAIR, OWN, ring.d_pair)
    got(7, R_NEAR_U, OWN, ring.d_down)
    got(8, R_NEAR_D, OWN, ring.d_up)
    for t in range(OWN):
        total = partial(i, p, t)
        for term in (R_PAIR, R_NEAR_U, R_NEAR_D):
            total = total + rbuf[term + t].astype(F32)
        out(t, total)
    yield


def kernel(
    scaling, table, features, weight, tiles, out_grad, activated, weight_grad, feature_grad,
    T, S0, S1, F0, F1, CS0, CS1, CR0, CR1, AS0, AS1, AR0, AR1, G0, G1, BS0, BS1, BR0, BR1,
    AGG0, AGG1, PG, WT, WA, WP, WB, WC,
    tile_sem, gf_s, gf_r, cx_s, cx_r, rf_s, rf_r, gb_s, gb_r, co_s, co_r, rb_s, rb_r,
    wa_s, wa_r, wb_s, wb_r, wc_s, wc_r,
):
    S, F, CS, CR, AS, AR = (S0, S1), (F0, F1), (CS0, CS1), (CR0, CR1), (AS0, AS1), (AR0, AR1)
    G, BS, BR, AGG = (G0, G1), (BS0, BS1), (BR0, BR1), (AGG0, AGG1)
    row, col = lax.axis_index("row"), lax.axis_index("col")
    x, zl = row // 2, lax.rem(row, 2)
    zh, y, co = col // 8, lax.rem(col, 8) // 2, lax.rem(col, 2)
    row_ring = Ring(x, zl, lambda i, p: (i * 2 + p, col), lambda i, p: i * 2 + p)
    col_ring = Ring(y, zh, lambda i, p: (row, p * 8 + i * 2 + co), lambda i, p: p * 8 + i * 2 + co)
    partner = (row, zh * 8 + y * 2 + 1 - co)
    sent = []

    loads = []
    for n in range(4):
        span = pl.ds(n * (SLOTS // 4), SLOTS // 4)
        loads.append(pltpu.make_async_copy(tiles.at[span], T.at[span], tile_sem.at[n]))
        loads[-1].start()

    barrier = pltpu.get_barrier_semaphore()

    def greet_col(k, c):
        pl.semaphore_signal(barrier, inc=1, device_id=(row, lax.rem(col + k, 16)), device_id_type=MESH)
        return c

    def greet_row(k, c):
        pl.semaphore_signal(barrier, inc=1, device_id=(lax.rem(row + k, 8), col), device_id_type=MESH)
        return c

    lax.fori_loop(1, 16, greet_col, 0)
    lax.fori_loop(1, 8, greet_row, 0)
    for h in range(2):
        for t in range(OWN):
            F[h][row * OWN + t] = features[t * TILE:(t + 1) * TILE, h * TILE:(h + 1) * TILE]
        S[h][SLOTS] = jnp.zeros((TILE, TILE), F32)
    pl.semaphore_wait(barrier, 22)

    def spread(h, source, prev, src, contract, first=0, last=SLOTS):
        def step(k, c):
            term = lax.dot_general(
                T[k], source[table[src + k]], (((contract,), (0,)), ((), ())), preferred_element_type=F32
            )
            S[h][k] = S[h][table[prev + k]] + term
            return c

        lax.fori_loop(first, last, step, 0, unroll=16)

    def core_exchange(h):
        for b in range(8):
            for t in range(OWN):
                CS[h][b * OWN + t] = S[h][table[LAST_F + (b * 2 + 1 - co) * OWN + t]].astype(BF16)
        sent.append(send(CS[h], CR[h], cx_s.at[h], cx_r.at[h], partner))

    def forward_term(h, i, p, t):
        b = p * 4 + i
        return S[h][table[LAST_F + (b * 2 + co) * OWN + t]] + CR[h][b * OWN + t].astype(F32)

    def keep_aggregated(h, t, value):
        AGG[h][t * TILE:(t + 1) * TILE, :] = value.astype(BF16)

    gf = [gather(row_ring, F[h], gf_s.at[h], gf_r.at[h], sent) for h in range(2)]
    rf = [
        reduce(col_ring, functools.partial(forward_term, h), functools.partial(keep_aggregated, h),
               AS[h], AR[h], rf_s.at[h], rf_r.at[h], sent)
        for h in range(2)
    ]
    next(gf[0])
    next(gf[0])
    next(gf[1])
    next(gf[0])
    next(gf[1])
    for load in loads:
        load.wait()
    next(gf[0])
    spread(0, F[0], PREV_F, SRC_F, 1)
    core_exchange(0)
    next(gf[1])
    arrive(CR[0], cx_s.at[0], cx_r.at[0], partner)
    next(rf[0])
    next(gf[1])
    next(rf[0])
    spread(1, F[1], PREV_F, SRC_F, 1)
    core_exchange(1)
    next(rf[0])
    next(rf[0])
    arrive(CR[1], cx_s.at[1], cx_r.at[1], partner)
    next(rf[1])
    next(rf[1])
    next(rf[0])
    next(rf[1])
    next(rf[1])
    next(rf[1])

    def own_tile(t, c):
        rows = pl.ds(pl.multiple_of(t * TILE, TILE), TILE)
        pre = jnp.dot(AGG0[rows, :], weight[:TILE, :], preferred_element_type=F32)
        pre = pre + jnp.dot(AGG1[rows, :], weight[TILE:, :], preferred_element_type=F32)
        sigma = jax.nn.sigmoid(pre)
        activated[rows, :] = (pre * sigma).astype(BF16)
        grad = out_grad[rows, :].astype(F32) * (sigma * (1.0 + pre * (1.0 - sigma)))
        grad = grad.astype(BF16)
        PG[rows, :] = grad
        for h in range(2):
            back = lax.dot_general(
                grad, weight[h * TILE:(h + 1) * TILE, :], (((1,), (1,)), ((), ())), preferred_element_type=F32
            )
            G[h][col * OWN + t] = back.astype(BF16)
        return c

    lax.fori_loop(0, OWN, own_tile, 0, unroll=2)

    def to_partner(h):
        count = [0]

        def landed(place):
            what = G[h].at[pl.ds(col_ring.block(*place) * OWN, OWN)]
            n = count[0]
            count[0] += 1
            sent.append(send(what, what, co_s.at[h, n], co_r.at[h, n], partner))

        return landed

    def from_partner(h):
        r = col_ring
        places = [(r.i, r.p), (r.down, r.p), (r.up, r.p), (r.i, r.q), (r.far, r.p), (r.down, r.q), (r.up, r.q), (r.far, r.q)]
        for n, (i, p) in enumerate(places):
            arrive(G[h].at[pl.ds((p * 8 + i * 2 + 1 - co) * OWN, OWN)], co_s.at[h, n], co_r.at[h, n], partner)

    def backward_term(h, i, p, t):
        return S[h][table[LAST_B + (i * 2 + p) * OWN + t]]

    def keep_feature_grad(h, t, value):
        feature_grad[t * TILE:(t + 1) * TILE, h * TILE:(h + 1) * TILE] = value.astype(BF16)

    gb = [gather(col_ring, G[h], gb_s.at[h], gb_r.at[h], sent, to_partner(h)) for h in range(2)]
    rb = [
        reduce(row_ring, functools.partial(backward_term, h), functools.partial(keep_feature_grad, h),
               BS[h], BR[h], rb_s.at[h], rb_r.at[h], sent)
        for h in range(2)
    ]

    def weight_term():
        for h in range(2):
            WT[h * TILE:(h + 1) * TILE, :] = lax.dot_general(
                AGG[h][...], PG[...], (((0,), (0,)), ((), ())), preferred_element_type=F32
            )

        def go(k, c):
            to = lax.rem(col + k, 16)
            send(WT.at[pl.ds(to * 16, 16)], WA.at[col], wa_s.at[k], wa_r.at[k], (row, to))
            return c

        lax.fori_loop(1, 16, go, 0)

    def weight_row():
        WA[col] = WT[pl.ds(pl.multiple_of(col * 16, 16), 16), :]

        def got(k, c):
            fro = lax.rem(col + 16 - k, 16)
            arrive(WA.at[fro], wa_s.at[k], wa_r.at[k], (row, fro))
            return c

        lax.fori_loop(1, 16, got, 0)
        total = WA[0]
        for n in range(1, 16):
            total = total + WA[n]
        WP[...] = total
        WB[row] = total

        def go(k, c):
            to = lax.rem(row + k, 8)
            send(WP, WB.at[row], wb_s.at[k], wb_r.at[k], (to, col))
            return c

        lax.fori_loop(1, 8, go, 0)

    def weight_back():
        def got(k, c):
            fro = lax.rem(row + 8 - k, 8)
            arrive(WB.at[fro], wb_s.at[k], wb_r.at[k], (fro, col))
            return c

        lax.fori_loop(1, 8, got, 0)
        total = WB[0]
        for n in range(1, 8):
            total = total + WB[n]
        here = pl.ds(pl.multiple_of(col * 16, 16), 16)
        WC[here, :] = total * scaling

        def go(k, c):
            to = lax.rem(col + k, 16)
            send(WC.at[here], WC.at[here], wc_s.at[k], wc_r.at[k], (row, to))
            return c

        lax.fori_loop(1, 16, go, 0)

    def weight_end():
        def got(k, c):
            fro = lax.rem(col + 16 - k, 16)
            arrive(WC.at[pl.ds(fro * 16, 16)], wc_s.at[k], wc_r.at[k], (row, fro))
            return c

        lax.fori_loop(1, 16, got, 0)
        weight_grad[...] = WC[...]

    next(gb[0])
    weight_term()
    next(gb[0])
    next(gb[1])
    next(gb[0])
    next(gb[1])
    next(gb[0])
    weight_row()
    from_partner(0)
    spread(0, G[0], PREV_B, SRC_B, 0)
    next(gb[1])
    next(rb[0])
    weight_back()
    next(gb[1])
    next(rb[0])
    from_partner(1)
    spread(1, G[1], PREV_B, SRC_B, 0)
    next(rb[0])
    next(rb[1])
    next(rb[0])
    next(rb[1])
    next(rb[0])
    next(rb[1])
    next(rb[1])
    weight_end()
    next(rb[1])

    for copy in sent:
        copy.wait_send()

    def gone_col(k, c):
        pltpu.make_async_remote_copy(
            src_ref=WP, dst_ref=WP, send_sem=wa_s.at[k], recv_sem=wa_r.at[k], device_id=partner, device_id_type=MESH
        ).wait_send()
        pltpu.make_async_remote_copy(
            src_ref=WP, dst_ref=WP, send_sem=wc_s.at[k], recv_sem=wc_r.at[k], device_id=partner, device_id_type=MESH
        ).wait_send()
        return c

    def gone_row(k, c):
        pltpu.make_async_remote_copy(
            src_ref=WP, dst_ref=WP, send_sem=wb_s.at[k], recv_sem=wb_r.at[k], device_id=partner, device_id_type=MESH
        ).wait_send()
        return c

    lax.fori_loop(1, 16, gone_col, 0)
    lax.fori_loop(1, 8, gone_row, 0)


def links(place, live, groups):
    slot = jnp.arange(SLOTS, dtype=jnp.int32)
    before = (place[None, :] == place[:, None]) & (slot[None, :] < slot[:, None]) & live[None, :]
    previous = jnp.max(jnp.where(before, slot[None, :], -1), axis=1)
    group = jnp.arange(groups, dtype=jnp.int32)
    inside = (place[None, :] == group[:, None]) & live[None, :]
    last = jnp.max(jnp.where(inside, slot[None, :], -1), axis=1)
    return jnp.where(previous < 0, SLOTS, previous), jnp.where(last < 0, SLOTS, last)


def body(scaling, features, weight, tile_values, tile_coords, tile_counts, out_grad):
    coords = tile_coords[0, 0]
    live = jnp.arange(SLOTS, dtype=jnp.int32) < tile_counts[0, 0]
    tile_row, tile_col = coords[:, 0], coords[:, 1]
    prev_f, last_f = links(tile_row, live, ROW_TILES)
    prev_b, last_b = links(tile_col, live, COL_TILES)
    table = jnp.concatenate(
        [prev_f, jnp.where(live, tile_col, 0), last_f, prev_b, jnp.where(live, tile_row, 0), last_b]
    )
    rows, width = features.shape
    vmem = pl.BlockSpec(memory_space=pltpu.VMEM)
    tile = (TILE, TILE)

    def twice(count, kind=BF16):
        return [pltpu.VMEM((count,) + tile, kind)] * 2

    dma = pltpu.SemaphoreType.DMA
    return pl.pallas_call(
        functools.partial(kernel, scaling),
        out_shape=(
            jax.ShapeDtypeStruct((rows, width), BF16),
            jax.ShapeDtypeStruct((width, width), F32),
            jax.ShapeDtypeStruct((rows, width), BF16),
        ),
        in_specs=[
            pl.BlockSpec(memory_space=pltpu.SMEM), vmem, vmem, pl.BlockSpec(memory_space=pl.ANY), vmem,
        ],
        out_specs=(vmem, vmem, vmem),
        scratch_shapes=[
            pltpu.VMEM((SLOTS,) + tile, BF16),
            *twice(SLOTS + 1, F32), *twice(COL_TILES), *twice(32), *twice(32), *twice(R_TILES), *twice(R_TILES),
            *twice(ROW_TILES), *twice(R_TILES), *twice(R_TILES),
            pltpu.VMEM((rows, TILE), BF16), pltpu.VMEM((rows, TILE), BF16), pltpu.VMEM((rows, width), BF16),
            pltpu.VMEM((width, width), F32), pltpu.VMEM((16, 16, width), F32), pltpu.VMEM((16, width), F32),
            pltpu.VMEM((8, 16, width), F32), pltpu.VMEM((width, width), F32),
            dma((4,)), dma((2, 9)), dma((2, 9)), dma((2,)), dma((2,)), dma((2, 9)), dma((2, 9)),
            dma((2, 9)), dma((2, 9)), dma((2, 8)), dma((2, 8)), dma((2, 9)), dma((2, 9)),
            dma((16,)), dma((16,)), dma((8,)), dma((8,)), dma((16,)), dma((16,)),
        ],
        compiler_params=pltpu.CompilerParams(
            collective_id=0, has_side_effects=True, vmem_limit_bytes=62 << 20
        ),
    )(table, features, weight, tile_values[0, 0], out_grad)


def solution(mesh):
    nodes = 512 * mesh.shape["row"] * mesh.shape["col"]
    return jax.shard_map(
        functools.partial(body, float(nodes) ** -0.5),
        mesh=mesh,
        in_specs=(
            P(("row", "col"), None), P(), P("row", "col", None, None, None), P("row", "col", None, None),
            P("row", "col"), P(("row", "col"), None),
        ),
        out_specs=(P(("row", "col"), None), P(), P(("row", "col"), None)),
        check_vma=False,
    )
```

```python
import functools

import jax
import jax.numpy as jnp
from jax import lax
from jax.experimental import pallas as pl
from jax.experimental.pallas import tpu as pltpu
from jax.sharding import PartitionSpec as P

MESH = pl.DeviceIdType.MESH
TILE = 128
SLOTS = 192
ROW_TILES = 64
COL_TILES = 32
OWN = 4
HALF = 2
WIDE = 256
PREV_F, SRC_F, LAST_F, PREV_B, SRC_B, LAST_B = range(6)
R_FARP, R_NEARP_U, R_NEARP_D, R_FAR_U, R_FAR_D, R_NEAR_U, R_NEAR_D, R_PAIR = 0, 4, 8, 12, 14, 16, 20, 24
R_TILES = 28
F32 = jnp.float32
BF16 = jnp.bfloat16


def send(src, dst, ssem, rsem, device):
    copy = pltpu.make_async_remote_copy(
        src_ref=src, dst_ref=dst, send_sem=ssem, recv_sem=rsem, device_id=device, device_id_type=MESH
    )
    copy.start()
    return copy


def arrive(dst, ssem, rsem, device):
    pltpu.make_async_remote_copy(
        src_ref=dst, dst_ref=dst, send_sem=ssem, recv_sem=rsem, device_id=device, device_id_type=MESH
    ).wait_recv()


def run(steps, count):
    for _ in range(count):
        next(steps)


class Ring:
    def __init__(self, i, p, device, block):
        self.up, self.down, self.far = lax.rem(i + 1, 4), lax.rem(i + 3, 4), lax.rem(i + 2, 4)
        self.i, self.p, self.q = i, p, 1 - p
        self.d_up, self.d_down, self.d_pair = device(self.up, p), device(self.down, p), device(i, self.q)
        self.block = block


def gather(ring, buf, ss, rs, sent, landed=lambda name: None):
    i, p, q, up, down, far = ring.i, ring.p, ring.q, ring.up, ring.down, ring.far

    def part(i, p, first=0, count=OWN):
        return buf.at[pl.ds(ring.block(i, p) * OWN + first, count)]

    def go(n, what, device):
        sent.append(send(what, what, ss.at[n], rs.at[n], device))

    def got(n, what, device):
        arrive(what, ss.at[n], rs.at[n], device)

    go(0, part(i, p, 0, HALF), ring.d_up)
    go(1, part(i, p, HALF, HALF), ring.d_down)
    go(4, part(i, p), ring.d_pair)
    go(2, part(i, p, HALF, HALF), ring.d_up)
    go(3, part(i, p, 0, HALF), ring.d_down)
    landed((i, p))
    yield
    got(0, part(down, p, 0, HALF), ring.d_down)
    go(5, part(down, p, 0, HALF), ring.d_up)
    got(1, part(up, p, HALF, HALF), ring.d_up)
    go(6, part(up, p, HALF, HALF), ring.d_down)
    yield
    got(4, part(i, q), ring.d_pair)
    go(7, part(i, q), ring.d_up)
    go(8, part(i, q), ring.d_down)
    landed((i, q))
    got(2, part(down, p, HALF, HALF), ring.d_down)
    landed((down, p))
    got(3, part(up, p, 0, HALF), ring.d_up)
    landed((up, p))
    yield
    got(5, part(far, p, 0, HALF), ring.d_down)
    go(9, part(far, p, 0, HALF), ring.d_pair)
    got(6, part(far, p, HALF, HALF), ring.d_up)
    go(10, part(far, p, HALF, HALF), ring.d_pair)
    landed((far, p))
    yield
    got(7, part(down, q), ring.d_down)
    landed((down, q))
    got(8, part(up, q), ring.d_up)
    landed((up, q))
    yield
    got(9, part(far, q, 0, HALF), ring.d_pair)
    got(10, part(far, q, HALF, HALF), ring.d_pair)
    landed((far, q))
    yield


def reduce(ring, partial, out, sbuf, rbuf, ss, rs, sent):
    i, p, q, up, down, far = ring.i, ring.p, ring.q, ring.up, ring.down, ring.far

    def go(n, first, count, device):
        sent.append(
            send(sbuf.at[pl.ds(first, count)], rbuf.at[pl.ds(first, count)], ss.at[n], rs.at[n], device)
        )

    def got(n, first, count, device):
        arrive(rbuf.at[pl.ds(first, count)], ss.at[n], rs.at[n], device)

    def put(first, block, tiles=range(OWN), terms=()):
        for n, t in enumerate(tiles):
            total = partial(*block, t)
            for term in terms:
                total = total + rbuf[term + n].astype(F32)
            sbuf[first + n] = total.astype(BF16)

    put(R_FARP, (far, q))
    go(0, R_FARP, HALF, ring.d_pair)
    go(1, R_FARP + HALF, HALF, ring.d_pair)
    put(R_NEARP_U, (up, q))
    go(2, R_NEARP_U, OWN, ring.d_up)
    put(R_NEARP_D, (down, q))
    go(3, R_NEARP_D, OWN, ring.d_down)
    put(R_NEAR_U + HALF, (up, p), (2, 3))
    go(4, R_NEAR_U + HALF, HALF, ring.d_up)
    put(R_NEAR_D, (down, p), (0, 1))
    go(5, R_NEAR_D, HALF, ring.d_down)
    yield
    got(0, R_FARP, HALF, ring.d_pair)
    put(R_FAR_U, (far, p), (0, 1), (R_FARP,))
    go(6, R_FAR_U, HALF, ring.d_up)
    got(1, R_FARP + HALF, HALF, ring.d_pair)
    put(R_FAR_D, (far, p), (2, 3), (R_FARP + HALF,))
    go(7, R_FAR_D, HALF, ring.d_down)
    yield
    got(2, R_NEARP_U, OWN, ring.d_down)
    got(3, R_NEARP_D, OWN, ring.d_up)
    put(R_PAIR, (i, q), range(OWN), (R_NEARP_U, R_NEARP_D))
    go(8, R_PAIR, OWN, ring.d_pair)
    yield
    got(6, R_FAR_U, HALF, ring.d_down)
    put(R_NEAR_U, (up, p), (0, 1), (R_FAR_U,))
    go(9, R_NEAR_U, HALF, ring.d_up)
    got(7, R_FAR_D, HALF, ring.d_up)
    put(R_NEAR_D + HALF, (down, p), (2, 3), (R_FAR_D,))
    go(10, R_NEAR_D + HALF, HALF, ring.d_down)
    yield
    got(4, R_NEAR_U + HALF, HALF, ring.d_down)
    got(5, R_NEAR_D, HALF, ring.d_up)
    got(8, R_PAIR, OWN, ring.d_pair)
    got(9, R_NEAR_U, HALF, ring.d_down)
    got(10, R_NEAR_D + HALF, HALF, ring.d_up)
    for t in range(OWN):
        total = partial(i, p, t)
        for term in (R_PAIR, R_NEAR_U, R_NEAR_D):
            total = total + rbuf[term + t].astype(F32)
        out(t, total)
    yield


def make_table(coords, count, out):
    first = lax.broadcasted_iota(jnp.int32, (WIDE, WIDE), 0)
    second = lax.broadcasted_iota(jnp.int32, (WIDE, WIDE), 1)
    out[...] = jnp.zeros_like(out)
    pad = jnp.zeros((1, WIDE - SLOTS), jnp.int32)
    lane = lax.broadcasted_iota(jnp.int32, (1, WIDE), 1)
    for group, source, rows in ((0, 1, (PREV_F, SRC_F, LAST_F)), (1, 0, (PREV_B, SRC_B, LAST_B))):
        place = jnp.concatenate([coords[group:group + 1, :], pad], axis=1)
        taken = jnp.concatenate([coords[source:source + 1, :], pad], axis=1)
        along = jnp.broadcast_to(place, (WIDE, WIDE))
        across = along.T
        before = jnp.where((across == along) & (first < second) & (first < count), first, -1)
        previous = jnp.max(before, axis=0, keepdims=True)
        inside = jnp.where((across == second) & (first < count), first, -1)
        last = jnp.max(inside, axis=0, keepdims=True)
        out[rows[0]:rows[0] + 1, :] = jnp.where(previous < 0, SLOTS, previous)
        out[rows[1]:rows[1] + 1, :] = jnp.where(lane < count, taken, 0)
        out[rows[2]:rows[2] + 1, :] = jnp.where(last < 0, SLOTS, last)


def kernel(
    scaling, count, coords, features, weight, tiles, out_grad, activated, weight_grad, feature_grad,
    T, S0, S1, F0, F1, CS0, CS1, CR0, CR1, AS0, AS1, AR0, AR1, G0, G1, BS0, BS1, BR0, BR1,
    AGG0, AGG1, PG, WT, WA, WP, WB, WC,
    TABLE, table, table_sem, tile_sem, gf_s, gf_r, cx_s, cx_r, rf_s, rf_r, gb_s, gb_r, co_s, co_r, rb_s, rb_r,
    wa_s, wa_r, wb_s, wb_r, wc_s, wc_r,
):
    S, F, CS, CR, AS, AR = (S0, S1), (F0, F1), (CS0, CS1), (CR0, CR1), (AS0, AS1), (AR0, AR1)
    G, BS, BR, AGG = (G0, G1), (BS0, BS1), (BR0, BR1), (AGG0, AGG1)
    row, col = lax.axis_index("row"), lax.axis_index("col")
    x, zl = row // 2, lax.rem(row, 2)
    zh, y, co = col // 8, lax.rem(col, 8) // 2, lax.rem(col, 2)
    row_ring = Ring(x, zl, lambda i, p: (i * 2 + p, col), lambda i, p: i * 2 + p)
    col_ring = Ring(y, zh, lambda i, p: (row, p * 8 + i * 2 + co), lambda i, p: p * 8 + i * 2 + co)
    partner = (row, zh * 8 + y * 2 + 1 - co)
    sent = []

    loads = []
    for n in range(4):
        span = pl.ds(n * (SLOTS // 4), SLOTS // 4)
        loads.append(pltpu.make_async_copy(tiles.at[span], T.at[span], tile_sem.at[n]))
        loads[-1].start()

    barrier = pltpu.get_barrier_semaphore()

    def greet_col(k, c):
        pl.semaphore_signal(barrier, inc=1, device_id=(row, lax.rem(col + k, 16)), device_id_type=MESH)
        return c

    def greet_row(k, c):
        pl.semaphore_signal(barrier, inc=1, device_id=(lax.rem(row + k, 8), col), device_id_type=MESH)
        return c

    lax.fori_loop(1, 16, greet_col, 0)
    lax.fori_loop(1, 8, greet_row, 0)
    for h in range(2):
        for t in range(OWN):
            F[h][row * OWN + t] = features[t * TILE:(t + 1) * TILE, h * TILE:(h + 1) * TILE]
        S[h][SLOTS] = jnp.zeros((TILE, TILE), F32)
    make_table(coords, count[0, 0], TABLE)
    table_copy = pltpu.make_async_copy(TABLE, table, table_sem)
    table_copy.start()
    pl.semaphore_wait(barrier, 22)

    def spread(h, source, prev, src, contract, first=0, last=SLOTS):
        def step(k, c):
            term = lax.dot_general(
                T[k], source[table[src, k]], (((contract,), (0,)), ((), ())), preferred_element_type=F32
            )
            S[h][k] = S[h][table[prev, k]] + term
            return c

        lax.fori_loop(first, last, step, 0, unroll=32)

    def core_exchange(h):
        for b in range(8):
            for t in range(OWN):
                CS[h][b * OWN + t] = S[h][table[LAST_F, (b * 2 + 1 - co) * OWN + t]].astype(BF16)
        sent.append(send(CS[h], CR[h], cx_s.at[h], cx_r.at[h], partner))

    def forward_term(h, i, p, t):
        b = p * 4 + i
        return S[h][table[LAST_F, (b * 2 + co) * OWN + t]] + CR[h][b * OWN + t].astype(F32)

    def keep_aggregated(h, t, value):
        AGG[h][t * TILE:(t + 1) * TILE, :] = value.astype(BF16)

    gf = [gather(row_ring, F[h], gf_s.at[h], gf_r.at[h], sent) for h in range(2)]
    rf = [
        reduce(col_ring, functools.partial(forward_term, h), functools.partial(keep_aggregated, h),
               AS[h], AR[h], rf_s.at[h], rf_r.at[h], sent)
        for h in range(2)
    ]
    run(gf[0], 3)
    run(gf[1], 1)
    run(gf[0], 2)
    run(gf[1], 2)
    run(gf[0], 1)
    table_copy.wait()
    for load in loads:
        load.wait()
    spread(0, F[0], PREV_F, SRC_F, 1, 0, 128)
    run(gf[1], 1)
    spread(0, F[0], PREV_F, SRC_F, 1, 128)
    core_exchange(0)
    run(gf[1], 1)
    arrive(CR[0], cx_s.at[0], cx_r.at[0], partner)
    run(rf[0], 1)
    run(gf[1], 1)
    spread(1, F[1], PREV_F, SRC_F, 1, 0, 96)
    run(rf[0], 2)
    spread(1, F[1], PREV_F, SRC_F, 1, 96)
    core_exchange(1)
    run(rf[0], 1)
    arrive(CR[1], cx_s.at[1], cx_r.at[1], partner)
    run(rf[1], 1)
    run(rf[0], 1)
    run(rf[1], 4)

    def own_tile(t, c):
        rows = pl.ds(pl.multiple_of(t * TILE, TILE), TILE)
        pre = jnp.dot(AGG0[rows, :], weight[:TILE, :], preferred_element_type=F32)
        pre = pre + jnp.dot(AGG1[rows, :], weight[TILE:, :], preferred_element_type=F32)
        sigma = jax.nn.sigmoid(pre)
        activated[rows, :] = (pre * sigma).astype(BF16)
        grad = out_grad[rows, :].astype(F32) * (sigma * (1.0 + pre * (1.0 - sigma)))
        grad = grad.astype(BF16)
        PG[rows, :] = grad
        for h in range(2):
            back = lax.dot_general(
                grad, weight[h * TILE:(h + 1) * TILE, :], (((1,), (1,)), ((), ())), preferred_element_type=F32
            )
            G[h][col * OWN + t] = back.astype(BF16)
        return c

    lax.fori_loop(0, OWN, own_tile, 0, unroll=2)

    def to_partner(h):
        count = [0]

        def landed(place):
            what = G[h].at[pl.ds(col_ring.block(*place) * OWN, OWN)]
            n = count[0]
            count[0] += 1
            sent.append(send(what, what, co_s.at[h, n], co_r.at[h, n], partner))

        return landed

    def from_partner(h):
        r = col_ring
        places = [(r.i, r.p), (r.i, r.q), (r.down, r.p), (r.up, r.p), (r.far, r.p), (r.down, r.q), (r.up, r.q), (r.far, r.q)]
        for n, (i, p) in enumerate(places):
            arrive(G[h].at[pl.ds((p * 8 + i * 2 + 1 - co) * OWN, OWN)], co_s.at[h, n], co_r.at[h, n], partner)

    def backward_term(h, i, p, t):
        return S[h][table[LAST_B, (i * 2 + p) * OWN + t]]

    def keep_feature_grad(h, t, value):
        feature_grad[t * TILE:(t + 1) * TILE, h * TILE:(h + 1) * TILE] = value.astype(BF16)

    gb = [gather(col_ring, G[h], gb_s.at[h], gb_r.at[h], sent, to_partner(h)) for h in range(2)]
    rb = [
        reduce(row_ring, functools.partial(backward_term, h), functools.partial(keep_feature_grad, h),
               BS[h], BR[h], rb_s.at[h], rb_r.at[h], sent)
        for h in range(2)
    ]

    def weight_term():
        for h in range(2):
            WT[h * TILE:(h + 1) * TILE, :] = lax.dot_general(
                AGG[h][...], PG[...], (((0,), (0,)), ((), ())), preferred_element_type=F32
            )

    def weight_send():
        def go(k, c):
            to = lax.rem(col + k, 16)
            send(WT.at[pl.ds(to * 16, 16)], WA.at[col], wa_s.at[k], wa_r.at[k], (row, to))
            return c

        lax.fori_loop(1, 16, go, 0)

    def weight_row():
        WA[col] = WT[pl.ds(pl.multiple_of(col * 16, 16), 16), :]

        def got(k, c):
            fro = lax.rem(col + 16 - k, 16)
            arrive(WA.at[fro], wa_s.at[k], wa_r.at[k], (row, fro))
            return c

        lax.fori_loop(1, 16, got, 0)
        total = WA[0]
        for n in range(1, 16):
            total = total + WA[n]
        WP[...] = total
        WB[row] = total

        def go(k, c):
            to = lax.rem(row + k, 8)
            send(WP, WB.at[row], wb_s.at[k], wb_r.at[k], (to, col))
            return c

        lax.fori_loop(1, 8, go, 0)

    def weight_back():
        def got(k, c):
            fro = lax.rem(row + 8 - k, 8)
            arrive(WB.at[fro], wb_s.at[k], wb_r.at[k], (fro, col))
            return c

        lax.fori_loop(1, 8, got, 0)
        total = WB[0]
        for n in range(1, 8):
            total = total + WB[n]
        here = pl.ds(pl.multiple_of(col * 16, 16), 16)
        WC[here, :] = total * scaling

        def go(k, c):
            to = lax.rem(col + k, 16)
            send(WC.at[here], WC.at[here], wc_s.at[k], wc_r.at[k], (row, to))
            return c

        lax.fori_loop(1, 16, go, 0)

    def weight_end():
        def got(k, c):
            fro = lax.rem(col + 16 - k, 16)
            arrive(WC.at[pl.ds(fro * 16, 16)], wc_s.at[k], wc_r.at[k], (row, fro))
            return c

        lax.fori_loop(1, 16, got, 0)
        weight_grad[...] = WC[...]

    run(gb[0], 1)
    weight_term()
    run(gb[0], 2)
    run(gb[1], 1)
    weight_send()
    run(gb[0], 2)
    run(gb[1], 2)
    run(gb[0], 1)
    from_partner(0)
    spread(0, G[0], PREV_B, SRC_B, 0, 0, 128)
    run(gb[1], 1)
    spread(0, G[0], PREV_B, SRC_B, 0, 128)
    run(rb[0], 1)
    weight_row()
    run(gb[1], 2)
    run(rb[0], 1)
    from_partner(1)
    run(rb[0], 1)
    spread(1, G[1], PREV_B, SRC_B, 0, 0, 96)
    run(rb[0], 1)
    spread(1, G[1], PREV_B, SRC_B, 0, 96)
    run(rb[1], 1)
    weight_back()
    run(rb[0], 1)
    run(rb[1], 3)
    weight_end()
    run(rb[1], 1)

    for copy in sent:
        copy.wait_send()

    def gone_col(k, c):
        pltpu.make_async_remote_copy(
            src_ref=WP, dst_ref=WP, send_sem=wa_s.at[k], recv_sem=wa_r.at[k], device_id=partner, device_id_type=MESH
        ).wait_send()
        pltpu.make_async_remote_copy(
            src_ref=WP, dst_ref=WP, send_sem=wc_s.at[k], recv_sem=wc_r.at[k], device_id=partner, device_id_type=MESH
        ).wait_send()
        return c

    def gone_row(k, c):
        pltpu.make_async_remote_copy(
            src_ref=WP, dst_ref=WP, send_sem=wb_s.at[k], recv_sem=wb_r.at[k], device_id=partner, device_id_type=MESH
        ).wait_send()
        return c

    lax.fori_loop(1, 16, gone_col, 0)
    lax.fori_loop(1, 8, gone_row, 0)


def copy_kernel(*refs):
    count = len(refs) // 2
    for n in range(count):
        refs[count + n][...] = refs[n][...]


def keep(*arrays):
    where = pl.BlockSpec(memory_space=pltpu.VMEM)
    return pl.pallas_call(
        copy_kernel,
        out_shape=tuple(jax.ShapeDtypeStruct(a.shape, a.dtype) for a in arrays),
        in_specs=[where] * len(arrays),
        out_specs=(where,) * len(arrays),
    )(*arrays)


def body(scaling, features, weight, tile_values, tile_coords, tile_counts, out_grad):
    rows, width = features.shape
    vmem = pl.BlockSpec(memory_space=pltpu.VMEM)
    tile = (TILE, TILE)

    def twice(count, kind=BF16):
        return [pltpu.VMEM((count,) + tile, kind)] * 2

    dma = pltpu.SemaphoreType.DMA
    outs = pl.pallas_call(
        functools.partial(kernel, scaling),
        out_shape=(
            jax.ShapeDtypeStruct((rows, width), BF16),
            jax.ShapeDtypeStruct((width, width), F32),
            jax.ShapeDtypeStruct((rows, width), BF16),
        ),
        in_specs=[
            pl.BlockSpec(memory_space=pltpu.SMEM), vmem, vmem, vmem, pl.BlockSpec(memory_space=pl.ANY), vmem,
        ],
        out_specs=(vmem, vmem, vmem),
        scratch_shapes=[
            pltpu.VMEM((SLOTS,) + tile, BF16),
            *twice(SLOTS + 1, F32), *twice(COL_TILES), *twice(32), *twice(32), *twice(R_TILES), *twice(R_TILES),
            *twice(ROW_TILES), *twice(R_TILES), *twice(R_TILES),
            pltpu.VMEM((rows, TILE), BF16), pltpu.VMEM((rows, TILE), BF16), pltpu.VMEM((rows, width), BF16),
            pltpu.VMEM((width, width), F32), pltpu.VMEM((16, 16, width), F32), pltpu.VMEM((16, width), F32),
            pltpu.VMEM((8, 16, width), F32), pltpu.VMEM((width, width), F32),
            pltpu.VMEM((8, WIDE), jnp.int32), pltpu.SMEM((8, WIDE), jnp.int32), dma(()),
            dma((4,)), dma((2, 11)), dma((2, 11)), dma((2,)), dma((2,)), dma((2, 11)), dma((2, 11)),
            dma((2, 11)), dma((2, 11)), dma((2, 8)), dma((2, 8)), dma((2, 11)), dma((2, 11)),
            dma((16,)), dma((16,)), dma((8,)), dma((8,)), dma((16,)), dma((16,)),
        ],
        compiler_params=pltpu.CompilerParams(
            collective_id=0, has_side_effects=True, vmem_limit_bytes=62 << 20
        ),
    )(tile_counts, tile_coords[0, 0].T, features, weight, tile_values[0, 0], out_grad)
    return keep(*outs)


def solution(mesh):
    nodes = 512 * mesh.shape["row"] * mesh.shape["col"]
    return jax.shard_map(
        functools.partial(body, float(nodes) ** -0.5),
        mesh=mesh,
        in_specs=(
            P(("row", "col"), None), P(), P("row", "col", None, None, None), P("row", "col", None, None),
            P("row", "col"), P(("row", "col"), None),
        ),
        out_specs=(P(("row", "col"), None), P(), P(("row", "col"), None)),
        check_vma=False,
    )
```

```python
import functools

import jax
import jax.numpy as jnp
from jax import lax
from jax.experimental import pallas as pl
from jax.experimental.pallas import tpu as pltpu
from jax.sharding import PartitionSpec as P

MESH = pl.DeviceIdType.MESH
TILE = 128
SLOTS = 192
ROW_TILES = 64
COL_TILES = 32
OWN = 4
HALF = 2
WIDE = 256
PREV_F, SRC_F, LAST_F, PREV_B, SRC_B, LAST_B = range(6)
R_FARP, R_NEARP_U, R_NEARP_D, R_FAR_U, R_FAR_D, R_NEAR_U, R_NEAR_D, R_PAIR = 0, 4, 8, 12, 14, 16, 20, 24
R_TILES = 28
F32 = jnp.float32
BF16 = jnp.bfloat16


def send(src, dst, ssem, rsem, device):
    copy = pltpu.make_async_remote_copy(
        src_ref=src, dst_ref=dst, send_sem=ssem, recv_sem=rsem, device_id=device, device_id_type=MESH
    )
    copy.start()
    return copy


def arrive(dst, ssem, rsem, device):
    pltpu.make_async_remote_copy(
        src_ref=dst, dst_ref=dst, send_sem=ssem, recv_sem=rsem, device_id=device, device_id_type=MESH
    ).wait_recv()


def run(steps, count):
    for _ in range(count):
        next(steps)


class Ring:
    def __init__(self, i, p, device, block):
        self.up, self.down, self.far = lax.rem(i + 1, 4), lax.rem(i + 3, 4), lax.rem(i + 2, 4)
        self.i, self.p, self.q = i, p, 1 - p
        self.d_up, self.d_down, self.d_pair = device(self.up, p), device(self.down, p), device(i, self.q)
        self.block = block


def gather(ring, buf, ss, rs, sent, landed=lambda name: None):
    i, p, q, up, down, far = ring.i, ring.p, ring.q, ring.up, ring.down, ring.far

    def part(i, p, first=0, count=OWN):
        return buf.at[pl.ds(ring.block(i, p) * OWN + first, count)]

    def go(n, what, device):
        sent.append(send(what, what, ss.at[n], rs.at[n], device))

    def got(n, what, device):
        arrive(what, ss.at[n], rs.at[n], device)

    go(0, part(i, p, 0, HALF), ring.d_up)
    go(1, part(i, p, HALF, HALF), ring.d_down)
    go(4, part(i, p), ring.d_pair)
    go(2, part(i, p, HALF, HALF), ring.d_up)
    go(3, part(i, p, 0, HALF), ring.d_down)
    landed((i, p))
    yield
    got(0, part(down, p, 0, HALF), ring.d_down)
    go(5, part(down, p, 0, HALF), ring.d_up)
    got(1, part(up, p, HALF, HALF), ring.d_up)
    go(6, part(up, p, HALF, HALF), ring.d_down)
    yield
    got(4, part(i, q), ring.d_pair)
    go(7, part(i, q), ring.d_up)
    go(8, part(i, q), ring.d_down)
    landed((i, q))
    got(2, part(down, p, HALF, HALF), ring.d_down)
    landed((down, p))
    got(3, part(up, p, 0, HALF), ring.d_up)
    landed((up, p))
    yield
    got(5, part(far, p, 0, HALF), ring.d_down)
    go(9, part(far, p, 0, HALF), ring.d_pair)
    got(6, part(far, p, HALF, HALF), ring.d_up)
    go(10, part(far, p, HALF, HALF), ring.d_pair)
    landed((far, p))
    yield
    got(7, part(down, q), ring.d_down)
    landed((down, q))
    got(8, part(up, q), ring.d_up)
    landed((up, q))
    yield
    got(9, part(far, q, 0, HALF), ring.d_pair)
    got(10, part(far, q, HALF, HALF), ring.d_pair)
    landed((far, q))
    yield


def reduce(ring, partial, out, sbuf, rbuf, ss, rs, sent):
    i, p, q, up, down, far = ring.i, ring.p, ring.q, ring.up, ring.down, ring.far

    def go(n, first, count, device):
        sent.append(
            send(sbuf.at[pl.ds(first, count)], rbuf.at[pl.ds(first, count)], ss.at[n], rs.at[n], device)
        )

    def got(n, first, count, device):
        arrive(rbuf.at[pl.ds(first, count)], ss.at[n], rs.at[n], device)

    def put(first, block, tiles=range(OWN), terms=()):
        for n, t in enumerate(tiles):
            total = partial(*block, t)
            for term in terms:
                total = total + rbuf[term + n].astype(F32)
            sbuf[first + n] = total.astype(BF16)

    put(R_FARP, (far, q))
    go(0, R_FARP, HALF, ring.d_pair)
    go(1, R_FARP + HALF, HALF, ring.d_pair)
    put(R_NEARP_U, (up, q))
    go(2, R_NEARP_U, OWN, ring.d_up)
    put(R_NEARP_D, (down, q))
    go(3, R_NEARP_D, OWN, ring.d_down)
    put(R_NEAR_U + HALF, (up, p), (2, 3))
    go(4, R_NEAR_U + HALF, HALF, ring.d_up)
    put(R_NEAR_D, (down, p), (0, 1))
    go(5, R_NEAR_D, HALF, ring.d_down)
    yield
    got(0, R_FARP, HALF, ring.d_pair)
    put(R_FAR_U, (far, p), (0, 1), (R_FARP,))
    go(6, R_FAR_U, HALF, ring.d_up)
    got(1, R_FARP + HALF, HALF, ring.d_pair)
    put(R_FAR_D, (far, p), (2, 3), (R_FARP + HALF,))
    go(7, R_FAR_D, HALF, ring.d_down)
    yield
    got(2, R_NEARP_U, OWN, ring.d_down)
    got(3, R_NEARP_D, OWN, ring.d_up)
    put(R_PAIR, (i, q), range(OWN), (R_NEARP_U, R_NEARP_D))
    go(8, R_PAIR, OWN, ring.d_pair)
    yield
    got(6, R_FAR_U, HALF, ring.d_down)
    put(R_NEAR_U, (up, p), (0, 1), (R_FAR_U,))
    go(9, R_NEAR_U, HALF, ring.d_up)
    got(7, R_FAR_D, HALF, ring.d_up)
    put(R_NEAR_D + HALF, (down, p), (2, 3), (R_FAR_D,))
    go(10, R_NEAR_D + HALF, HALF, ring.d_down)
    yield
    got(4, R_NEAR_U + HALF, HALF, ring.d_down)
    got(5, R_NEAR_D, HALF, ring.d_up)
    got(8, R_PAIR, OWN, ring.d_pair)
    got(9, R_NEAR_U, HALF, ring.d_down)
    got(10, R_NEAR_D + HALF, HALF, ring.d_up)
    for t in range(OWN):
        total = partial(i, p, t)
        for term in (R_PAIR, R_NEAR_U, R_NEAR_D):
            total = total + rbuf[term + t].astype(F32)
        out(t, total)
    yield


def make_table(coords, count, out):
    first = lax.broadcasted_iota(jnp.int32, (WIDE, WIDE), 0)
    second = lax.broadcasted_iota(jnp.int32, (WIDE, WIDE), 1)
    out[...] = jnp.zeros_like(out)
    pad = jnp.zeros((1, WIDE - SLOTS), jnp.int32)
    lane = lax.broadcasted_iota(jnp.int32, (1, WIDE), 1)
    for group, source, rows in ((0, 1, (PREV_F, SRC_F, LAST_F)), (1, 0, (PREV_B, SRC_B, LAST_B))):
        place = jnp.concatenate([coords[group:group + 1, :], pad], axis=1)
        taken = jnp.concatenate([coords[source:source + 1, :], pad], axis=1)
        along = jnp.broadcast_to(place, (WIDE, WIDE))
        across = along.T
        before = jnp.where((across == along) & (first < second) & (first < count), first, -1)
        previous = jnp.max(before, axis=0, keepdims=True)
        inside = jnp.where((across == second) & (first < count), first, -1)
        last = jnp.max(inside, axis=0, keepdims=True)
        out[rows[0]:rows[0] + 1, :] = jnp.where(previous < 0, SLOTS, previous)
        out[rows[1]:rows[1] + 1, :] = jnp.where(lane < count, taken, 0)
        out[rows[2]:rows[2] + 1, :] = jnp.where(last < 0, SLOTS, last)


def kernel(
    scaling, count, coords, features, weight_hbm, tiles, out_grad_hbm, activated, weight_grad, feature_grad,
    T, S0, S1, F0, F1, CS0, CS1, CR0, CR1, AS0, AS1, AR0, AR1, G0, G1, BS0, BS1, BR0, BR1,
    AGG0, AGG1, PG, WT, WX, WS, WA, WP, WB, WC, weight, out_grad, ACT, FG,
    TABLE, table, table_sem, own_sem, out_sem, tile_sem, gf_s, gf_r, cx_s, cx_r, rf_s, rf_r, gb_s, gb_r, co_s, co_r, rb_s, rb_r,
    wx_s, wx_r, wa_s, wa_r, wb_s, wb_r, wc_s, wc_r,
):
    S, F, CS, CR, AS, AR = (S0, S1), (F0, F1), (CS0, CS1), (CR0, CR1), (AS0, AS1), (AR0, AR1)
    G, BS, BR, AGG = (G0, G1), (BS0, BS1), (BR0, BR1), (AGG0, AGG1)
    row, col = lax.axis_index("row"), lax.axis_index("col")
    x, zl = row // 2, lax.rem(row, 2)
    zh, y, co = col // 8, lax.rem(col, 8) // 2, lax.rem(col, 2)
    row_ring = Ring(x, zl, lambda i, p: (i * 2 + p, col), lambda i, p: i * 2 + p)
    col_ring = Ring(y, zh, lambda i, p: (row, p * 8 + i * 2 + co), lambda i, p: p * 8 + i * 2 + co)
    partner = (row, zh * 8 + y * 2 + 1 - co)
    sent = []

    own_loads = []
    for h in range(2):
        for t in range(OWN):
            own_loads.append(
                pltpu.make_async_copy(
                    features.at[pl.ds(t * TILE, TILE), pl.ds(h * TILE, TILE)], F[h].at[row * OWN + t],
                    own_sem.at[h * OWN + t],
                )
            )
            own_loads[-1].start()
    loads = []
    for n in range(4):
        span = pl.ds(n * (SLOTS // 4), SLOTS // 4)
        loads.append(pltpu.make_async_copy(tiles.at[span], T.at[span], tile_sem.at[n]))
        loads[-1].start()

    for source, place in ((weight_hbm, weight), (out_grad_hbm, out_grad)):
        loads.append(pltpu.make_async_copy(source, place, tile_sem.at[len(loads)]))
        loads[-1].start()
    stores = []

    def store(source, place, n):
        stores.append(pltpu.make_async_copy(source, place, out_sem.at[n]))
        stores[-1].start()

    barrier = pltpu.get_barrier_semaphore()

    def greet(k, c):
        near = (row, lax.rem(col + 2 * k, 16))
        pl.semaphore_signal(barrier, inc=1, device_id=near, device_id_type=MESH)
        pl.semaphore_signal(barrier, inc=1, device_id=(lax.rem(row + k, 8), col), device_id_type=MESH)
        return c

    pl.semaphore_signal(barrier, inc=1, device_id=partner, device_id_type=MESH)
    lax.fori_loop(1, 8, greet, 0)
    for h in range(2):
        S[h][SLOTS] = jnp.zeros((TILE, TILE), F32)
    make_table(coords, count[0, 0], TABLE)
    table_copy = pltpu.make_async_copy(TABLE, table, table_sem)
    table_copy.start()
    for load in own_loads:
        load.wait()
    pl.semaphore_wait(barrier, 15)

    def spread(h, source, prev, src, contract, first=0, last=SLOTS):
        def step(k, c):
            term = lax.dot_general(
                T[k], source[table[src, k]], (((contract,), (0,)), ((), ())), preferred_element_type=F32
            )
            S[h][k] = S[h][table[prev, k]] + term
            return c

        lax.fori_loop(first, last, step, 0, unroll=32)

    def core_exchange(h):
        for b in range(8):
            for t in range(OWN):
                CS[h][b * OWN + t] = S[h][table[LAST_F, (b * 2 + 1 - co) * OWN + t]].astype(BF16)
        sent.append(send(CS[h], CR[h], cx_s.at[h], cx_r.at[h], partner))

    def forward_term(h, i, p, t):
        b = p * 4 + i
        return S[h][table[LAST_F, (b * 2 + co) * OWN + t]] + CR[h][b * OWN + t].astype(F32)

    def keep_aggregated(h, t, value):
        AGG[h][t * TILE:(t + 1) * TILE, :] = value.astype(BF16)

    gf = [gather(row_ring, F[h], gf_s.at[h], gf_r.at[h], sent) for h in range(2)]
    rf = [
        reduce(col_ring, functools.partial(forward_term, h), functools.partial(keep_aggregated, h),
               AS[h], AR[h], rf_s.at[h], rf_r.at[h], sent)
        for h in range(2)
    ]
    run(gf[0], 3)
    run(gf[1], 1)
    run(gf[0], 2)
    run(gf[1], 2)
    run(gf[0], 1)
    table_copy.wait()
    for load in loads:
        load.wait()
    spread(0, F[0], PREV_F, SRC_F, 1, 0, 128)
    run(gf[1], 1)
    spread(0, F[0], PREV_F, SRC_F, 1, 128)
    core_exchange(0)
    run(gf[1], 1)
    arrive(CR[0], cx_s.at[0], cx_r.at[0], partner)
    run(rf[0], 1)
    run(gf[1], 1)
    spread(1, F[1], PREV_F, SRC_F, 1, 0, 96)
    run(rf[0], 2)
    spread(1, F[1], PREV_F, SRC_F, 1, 96)
    core_exchange(1)
    run(rf[0], 1)
    arrive(CR[1], cx_s.at[1], cx_r.at[1], partner)
    run(rf[1], 1)
    run(rf[0], 1)
    run(rf[1], 4)

    def own_tile(t, c):
        rows = pl.ds(pl.multiple_of(t * TILE, TILE), TILE)
        pre = jnp.dot(AGG0[rows, :], weight[:TILE, :], preferred_element_type=F32)
        pre = pre + jnp.dot(AGG1[rows, :], weight[TILE:, :], preferred_element_type=F32)
        sigma = jax.nn.sigmoid(pre)
        ACT[rows, :] = (pre * sigma).astype(BF16)
        grad = out_grad[rows, :].astype(F32) * (sigma * (1.0 + pre * (1.0 - sigma)))
        grad = grad.astype(BF16)
        PG[rows, :] = grad
        for h in range(2):
            back = lax.dot_general(
                grad, weight[h * TILE:(h + 1) * TILE, :], (((1,), (1,)), ((), ())), preferred_element_type=F32
            )
            G[h][col * OWN + t] = back.astype(BF16)
        return c

    lax.fori_loop(0, OWN, own_tile, 0, unroll=2)

    def to_partner(h):
        count = [0]

        def landed(place):
            what = G[h].at[pl.ds(col_ring.block(*place) * OWN, OWN)]
            n = count[0]
            count[0] += 1
            sent.append(send(what, what, co_s.at[h, n], co_r.at[h, n], partner))

        return landed

    def from_partner(h):
        r = col_ring
        places = [(r.i, r.p), (r.i, r.q), (r.down, r.p), (r.up, r.p), (r.far, r.p), (r.down, r.q), (r.up, r.q), (r.far, r.q)]
        for n, (i, p) in enumerate(places):
            arrive(G[h].at[pl.ds((p * 8 + i * 2 + 1 - co) * OWN, OWN)], co_s.at[h, n], co_r.at[h, n], partner)

    def backward_term(h, i, p, t):
        return S[h][table[LAST_B, (i * 2 + p) * OWN + t]]

    def keep_feature_grad(h, t, value):
        FG[t * TILE:(t + 1) * TILE, h * TILE:(h + 1) * TILE] = value.astype(BF16)

    gb = [gather(col_ring, G[h], gb_s.at[h], gb_r.at[h], sent, to_partner(h)) for h in range(2)]
    rb = [
        reduce(row_ring, functools.partial(backward_term, h), functools.partial(keep_feature_grad, h),
               BS[h], BR[h], rb_s.at[h], rb_r.at[h], sent)
        for h in range(2)
    ]

    chip = col // 2
    half = pl.ds(pl.multiple_of(co * 128, 128), 128)
    other = pl.ds(pl.multiple_of((1 - co) * 128, 128), 128)
    here = pl.ds(pl.multiple_of(co * 128 + chip * 16, 16), 16)

    def weight_term():
        for h in range(2):
            WT[h * TILE:(h + 1) * TILE, :] = lax.dot_general(
                AGG[h][...], PG[...], (((0,), (0,)), ((), ())), preferred_element_type=F32
            )
        sent.append(send(WT.at[other], WX, wx_s.at[0], wx_r.at[0], partner))

    def weight_send():
        arrive(WX, wx_s.at[0], wx_r.at[0], partner)
        for n in range(8):
            WS[n] = WT[pl.ds(pl.multiple_of(co * 128 + n * 16, 16), 16), :] + WX[n * 16:(n + 1) * 16, :]
        WA[chip] = WS[chip]

        def go(k, c):
            to = lax.rem(chip + k, 8)
            send(WS.at[to], WA.at[chip], wa_s.at[k], wa_r.at[k], (row, to * 2 + co))
            return c

        lax.fori_loop(1, 8, go, 0)

    def weight_row():
        def got(k, c):
            fro = lax.rem(chip + 8 - k, 8)
            arrive(WA.at[fro], wa_s.at[k], wa_r.at[k], (row, fro * 2 + co))
            return c

        lax.fori_loop(1, 8, got, 0)
        total = WA[0]
        for n in range(1, 8):
            total = total + WA[n]
        WP[...] = total
        WB[row] = total

        def go(k, c):
            to = lax.rem(row + k, 8)
            send(WP, WB.at[row], wb_s.at[k], wb_r.at[k], (to, col))
            return c

        lax.fori_loop(1, 8, go, 0)

    def weight_back():
        def got(k, c):
            fro = lax.rem(row + 8 - k, 8)
            arrive(WB.at[fro], wb_s.at[k], wb_r.at[k], (fro, col))
            return c

        lax.fori_loop(1, 8, got, 0)
        total = WB[0]
        for n in range(1, 8):
            total = total + WB[n]
        WC[here, :] = total * scaling

        def go(k, c):
            to = lax.rem(chip + k, 8)
            send(WC.at[here], WC.at[here], wc_s.at[k], wc_r.at[k], (row, to * 2 + co))
            return c

        lax.fori_loop(1, 8, go, 0)

    def weight_share():
        def got(k, c):
            fro = lax.rem(chip + 8 - k, 8)
            arrive(WC.at[pl.ds(co * 128 + fro * 16, 16)], wc_s.at[k], wc_r.at[k], (row, fro * 2 + co))
            return c

        lax.fori_loop(1, 8, got, 0)
        sent.append(send(WC.at[half], WC.at[half], wx_s.at[1], wx_r.at[1], partner))

    def weight_end():
        arrive(WC.at[other], wx_s.at[1], wx_r.at[1], partner)
        store(WC, weight_grad, 1)

    run(gb[0], 1)
    store(ACT, activated, 0)
    weight_term()
    run(gb[0], 2)
    run(gb[1], 1)
    weight_send()
    run(gb[0], 2)
    run(gb[1], 2)
    run(gb[0], 1)
    from_partner(0)
    spread(0, G[0], PREV_B, SRC_B, 0, 0, 128)
    run(gb[1], 1)
    spread(0, G[0], PREV_B, SRC_B, 0, 128)
    run(rb[0], 1)
    weight_row()
    run(gb[1], 2)
    run(rb[0], 1)
    from_partner(1)
    run(rb[0], 1)
    spread(1, G[1], PREV_B, SRC_B, 0, 0, 96)
    run(rb[0], 1)
    spread(1, G[1], PREV_B, SRC_B, 0, 96)
    run(rb[1], 1)
    weight_back()
    run(rb[0], 1)
    run(rb[1], 1)
    weight_share()
    run(rb[1], 2)
    weight_end()
    run(rb[1], 1)
    store(FG, feature_grad, 2)
    for copy in stores:
        copy.wait()

    for copy in sent:
        copy.wait_send()

    def gone(k, c):
        for ss, rs in ((wa_s, wa_r), (wb_s, wb_r), (wc_s, wc_r)):
            pltpu.make_async_remote_copy(
                src_ref=WP, dst_ref=WP, send_sem=ss.at[k], recv_sem=rs.at[k], device_id=partner, device_id_type=MESH
            ).wait_send()
        return c

    lax.fori_loop(1, 8, gone, 0)


def copy_kernel(*refs):
    count = len(refs) // 2
    for n in range(count):
        refs[count + n][...] = refs[n][...]


def keep(*arrays):
    where = pl.BlockSpec(memory_space=pltpu.VMEM)
    return pl.pallas_call(
        copy_kernel,
        out_shape=tuple(jax.ShapeDtypeStruct(a.shape, a.dtype) for a in arrays),
        in_specs=[where] * len(arrays),
        out_specs=(where,) * len(arrays),
    )(*arrays)


def body(scaling, features, weight, tile_values, tile_coords, tile_counts, out_grad):
    rows, width = features.shape
    hbm = pl.BlockSpec(memory_space=pl.ANY)
    tile = (TILE, TILE)

    def twice(count, kind=BF16):
        return [pltpu.VMEM((count,) + tile, kind)] * 2

    dma = pltpu.SemaphoreType.DMA
    outs = pl.pallas_call(
        functools.partial(kernel, scaling),
        out_shape=(
            jax.ShapeDtypeStruct((rows, width), BF16),
            jax.ShapeDtypeStruct((width, width), F32),
            jax.ShapeDtypeStruct((rows, width), BF16),
        ),
        in_specs=[
            pl.BlockSpec(memory_space=pltpu.SMEM), pl.BlockSpec(memory_space=pltpu.VMEM), hbm, hbm, hbm, hbm,
        ],
        out_specs=(hbm, hbm, hbm),
        scratch_shapes=[
            pltpu.VMEM((SLOTS,) + tile, BF16),
            *twice(SLOTS + 1, F32), *twice(COL_TILES), *twice(32), *twice(32), *twice(R_TILES), *twice(R_TILES),
            *twice(ROW_TILES), *twice(R_TILES), *twice(R_TILES),
            pltpu.VMEM((rows, TILE), BF16), pltpu.VMEM((rows, TILE), BF16), pltpu.VMEM((rows, width), BF16),
            pltpu.VMEM((width, width), F32), pltpu.VMEM((width // 2, width), F32), pltpu.VMEM((8, 16, width), F32),
            pltpu.VMEM((8, 16, width), F32), pltpu.VMEM((16, width), F32), pltpu.VMEM((8, 16, width), F32),
            pltpu.VMEM((width, width), F32), pltpu.VMEM((width, width), BF16), pltpu.VMEM((rows, width), BF16),
            pltpu.VMEM((rows, width), BF16), pltpu.VMEM((rows, width), BF16),
            pltpu.VMEM((8, WIDE), jnp.int32), pltpu.SMEM((8, WIDE), jnp.int32), dma(()),
            dma((8,)), dma((3,)), dma((6,)), dma((2, 11)), dma((2, 11)), dma((2,)), dma((2,)), dma((2, 11)), dma((2, 11)),
            dma((2, 11)), dma((2, 11)), dma((2, 8)), dma((2, 8)), dma((2, 11)), dma((2, 11)),
            dma((2,)), dma((2,)), dma((8,)), dma((8,)), dma((8,)), dma((8,)), dma((8,)), dma((8,)),
        ],
        compiler_params=pltpu.CompilerParams(
            collective_id=0, has_side_effects=True, vmem_limit_bytes=62 << 20
        ),
    )(tile_counts, tile_coords[0, 0].T, features, weight, tile_values[0, 0], out_grad)
    return keep(*outs)


def solution(mesh):
    nodes = 512 * mesh.shape["row"] * mesh.shape["col"]
    return jax.shard_map(
        functools.partial(body, float(nodes) ** -0.5),
        mesh=mesh,
        in_specs=(
            P(("row", "col"), None), P(), P("row", "col", None, None, None), P("row", "col", None, None),
            P("row", "col"), P(("row", "col"), None),
        ),
        out_specs=(P(("row", "col"), None), P(), P(("row", "col"), None)),
        check_vma=False,
    )
```

```python
import functools

import jax
import jax.numpy as jnp
from jax import lax
from jax.experimental import pallas as pl
from jax.experimental.pallas import tpu as pltpu
from jax.sharding import PartitionSpec as P

MESH = pl.DeviceIdType.MESH
TILE = 128
SLOTS = 192
ROW_TILES = 64
COL_TILES = 32
OWN = 4
HALF = 2
WIDE = 256
PREV_F, SRC_F, LAST_F, PREV_B, SRC_B, LAST_B = range(6)
R_FARP, R_NEARP_U, R_NEARP_D, R_FAR_U, R_FAR_D, R_NEAR_U, R_NEAR_D, R_PAIR = 0, 4, 8, 12, 14, 16, 20, 24
R_TILES = 28
F32 = jnp.float32
BF16 = jnp.bfloat16


def send(src, dst, ssem, rsem, device):
    copy = pltpu.make_async_remote_copy(
        src_ref=src, dst_ref=dst, send_sem=ssem, recv_sem=rsem, device_id=device, device_id_type=MESH
    )
    copy.start()
    return copy


def arrive(dst, ssem, rsem, device):
    pltpu.make_async_remote_copy(
        src_ref=dst, dst_ref=dst, send_sem=ssem, recv_sem=rsem, device_id=device, device_id_type=MESH
    ).wait_recv()


def run(steps, count):
    for _ in range(count):
        next(steps)


class Ring:
    def __init__(self, i, p, device, block):
        self.up, self.down, self.far = lax.rem(i + 1, 4), lax.rem(i + 3, 4), lax.rem(i + 2, 4)
        self.i, self.p, self.q = i, p, 1 - p
        self.d_up, self.d_down, self.d_pair = device(self.up, p), device(self.down, p), device(i, self.q)
        self.block = block


def gather(ring, buf, ss, rs, sent, landed=lambda name: None):
    i, p, q, up, down, far = ring.i, ring.p, ring.q, ring.up, ring.down, ring.far

    def part(i, p, first=0, count=OWN):
        return buf.at[pl.ds(ring.block(i, p) * OWN + first, count)]

    def go(n, what, device):
        sent.append(send(what, what, ss.at[n], rs.at[n], device))

    def got(n, what, device):
        arrive(what, ss.at[n], rs.at[n], device)

    go(0, part(i, p, 0, HALF), ring.d_up)
    go(1, part(i, p, HALF, HALF), ring.d_down)
    go(4, part(i, p), ring.d_pair)
    go(2, part(i, p, HALF, HALF), ring.d_up)
    go(3, part(i, p, 0, HALF), ring.d_down)
    landed((i, p))
    yield
    got(0, part(down, p, 0, HALF), ring.d_down)
    go(5, part(down, p, 0, HALF), ring.d_up)
    got(1, part(up, p, HALF, HALF), ring.d_up)
    go(6, part(up, p, HALF, HALF), ring.d_down)
    yield
    got(4, part(i, q), ring.d_pair)
    go(7, part(i, q), ring.d_up)
    go(8, part(i, q), ring.d_down)
    landed((i, q))
    got(2, part(down, p, HALF, HALF), ring.d_down)
    landed((down, p))
    got(3, part(up, p, 0, HALF), ring.d_up)
    landed((up, p))
    yield
    got(5, part(far, p, 0, HALF), ring.d_down)
    go(9, part(far, p, 0, HALF), ring.d_pair)
    got(6, part(far, p, HALF, HALF), ring.d_up)
    go(10, part(far, p, HALF, HALF), ring.d_pair)
    landed((far, p))
    yield
    got(7, part(down, q), ring.d_down)
    landed((down, q))
    got(8, part(up, q), ring.d_up)
    landed((up, q))
    yield
    got(9, part(far, q, 0, HALF), ring.d_pair)
    got(10, part(far, q, HALF, HALF), ring.d_pair)
    landed((far, q))
    yield


def reduce(ring, partial, out, sbuf, rbuf, ss, rs, sent):
    i, p, q, up, down, far = ring.i, ring.p, ring.q, ring.up, ring.down, ring.far

    def go(n, first, count, device):
        sent.append(
            send(sbuf.at[pl.ds(first, count)], rbuf.at[pl.ds(first, count)], ss.at[n], rs.at[n], device)
        )

    def got(n, first, count, device):
        arrive(rbuf.at[pl.ds(first, count)], ss.at[n], rs.at[n], device)

    def put(first, block, tiles=range(OWN), terms=()):
        for n, t in enumerate(tiles):
            total = partial(*block, t)
            for term in terms:
                total = total + rbuf[term + n].astype(F32)
            sbuf[first + n] = total.astype(BF16)

    put(R_FARP, (far, q))
    go(0, R_FARP, HALF, ring.d_pair)
    go(1, R_FARP + HALF, HALF, ring.d_pair)
    put(R_NEARP_U, (up, q))
    go(2, R_NEARP_U, OWN, ring.d_up)
    put(R_NEARP_D, (down, q))
    go(3, R_NEARP_D, OWN, ring.d_down)
    put(R_NEAR_U + HALF, (up, p), (2, 3))
    go(4, R_NEAR_U + HALF, HALF, ring.d_up)
    put(R_NEAR_D, (down, p), (0, 1))
    go(5, R_NEAR_D, HALF, ring.d_down)
    yield
    got(0, R_FARP, HALF, ring.d_pair)
    put(R_FAR_U, (far, p), (0, 1), (R_FARP,))
    go(6, R_FAR_U, HALF, ring.d_up)
    got(1, R_FARP + HALF, HALF, ring.d_pair)
    put(R_FAR_D, (far, p), (2, 3), (R_FARP + HALF,))
    go(7, R_FAR_D, HALF, ring.d_down)
    yield
    got(2, R_NEARP_U, OWN, ring.d_down)
    got(3, R_NEARP_D, OWN, ring.d_up)
    put(R_PAIR, (i, q), range(OWN), (R_NEARP_U, R_NEARP_D))
    go(8, R_PAIR, OWN, ring.d_pair)
    yield
    got(6, R_FAR_U, HALF, ring.d_down)
    put(R_NEAR_U, (up, p), (0, 1), (R_FAR_U,))
    go(9, R_NEAR_U, HALF, ring.d_up)
    got(7, R_FAR_D, HALF, ring.d_up)
    put(R_NEAR_D + HALF, (down, p), (2, 3), (R_FAR_D,))
    go(10, R_NEAR_D + HALF, HALF, ring.d_down)
    yield
    got(4, R_NEAR_U + HALF, HALF, ring.d_down)
    got(5, R_NEAR_D, HALF, ring.d_up)
    got(8, R_PAIR, OWN, ring.d_pair)
    got(9, R_NEAR_U, HALF, ring.d_down)
    got(10, R_NEAR_D + HALF, HALF, ring.d_up)
    for t in range(OWN):
        total = partial(i, p, t)
        for term in (R_PAIR, R_NEAR_U, R_NEAR_D):
            total = total + rbuf[term + t].astype(F32)
        out(t, total)
    yield


def make_table(coords, count, out):
    first = lax.broadcasted_iota(jnp.int32, (WIDE, WIDE), 0)
    second = lax.broadcasted_iota(jnp.int32, (WIDE, WIDE), 1)
    out[...] = jnp.zeros_like(out)
    pad = jnp.zeros((1, WIDE - SLOTS), jnp.int32)
    lane = lax.broadcasted_iota(jnp.int32, (1, WIDE), 1)
    for group, source, rows in ((0, 1, (PREV_F, SRC_F, LAST_F)), (1, 0, (PREV_B, SRC_B, LAST_B))):
        place = jnp.concatenate([coords[group:group + 1, :], pad], axis=1)
        taken = jnp.concatenate([coords[source:source + 1, :], pad], axis=1)
        along = jnp.broadcast_to(place, (WIDE, WIDE))
        across = along.T
        before = jnp.where((across == along) & (first < second) & (first < count), first, -1)
        previous = jnp.max(before, axis=0, keepdims=True)
        inside = jnp.where((across == second) & (first < count), first, -1)
        last = jnp.max(inside, axis=0, keepdims=True)
        out[rows[0]:rows[0] + 1, :] = jnp.where(previous < 0, SLOTS, previous)
        out[rows[1]:rows[1] + 1, :] = jnp.where(lane < count, taken, 0)
        out[rows[2]:rows[2] + 1, :] = jnp.where(last < 0, SLOTS, last)


def kernel(
    scaling, count, coords, features, weight_hbm, tiles, out_grad_hbm, activated, weight_grad, feature_grad,
    T, S0, S1, F0, F1, CS0, CS1, CR0, CR1, AS0, AS1, AR0, AR1, G0, G1, BS0, BS1, BR0, BR1,
    AGG0, AGG1, PG, WT, WX, WS, WA, WP, WB, WC, weight, out_grad, ACT, FG,
    TABLE, table, table_sem, own_sem, out_sem, tile_sem, gf_s, gf_r, cx_s, cx_r, rf_s, rf_r, gb_s, gb_r, co_s, co_r, rb_s, rb_r,
    wx_s, wx_r, wa_s, wa_r, wb_s, wb_r, wc_s, wc_r,
):
    S, F, CS, CR, AS, AR = (S0, S1), (F0, F1), (CS0, CS1), (CR0, CR1), (AS0, AS1), (AR0, AR1)
    G, BS, BR, AGG = (G0, G1), (BS0, BS1), (BR0, BR1), (AGG0, AGG1)
    row, col = lax.axis_index("row"), lax.axis_index("col")
    x, zl = row // 2, lax.rem(row, 2)
    zh, y, co = col // 8, lax.rem(col, 8) // 2, lax.rem(col, 2)
    row_ring = Ring(x, zl, lambda i, p: (i * 2 + p, col), lambda i, p: i * 2 + p)
    col_ring = Ring(y, zh, lambda i, p: (row, p * 8 + i * 2 + co), lambda i, p: p * 8 + i * 2 + co)
    partner = (row, zh * 8 + y * 2 + 1 - co)
    sent = []

    own_loads = []
    for h in range(2):
        for t in range(OWN):
            own_loads.append(
                pltpu.make_async_copy(
                    features.at[pl.ds(t * TILE, TILE), pl.ds(h * TILE, TILE)], F[h].at[row * OWN + t],
                    own_sem.at[h * OWN + t],
                )
            )
            own_loads[-1].start()
    loads = []
    for n in range(4):
        span = pl.ds(n * (SLOTS // 4), SLOTS // 4)
        loads.append(pltpu.make_async_copy(tiles.at[span], T.at[span], tile_sem.at[n]))
        loads[-1].start()

    for source, place in ((weight_hbm, weight), (out_grad_hbm, out_grad)):
        loads.append(pltpu.make_async_copy(source, place, tile_sem.at[len(loads)]))
        loads[-1].start()
    stores = []

    def store(source, place, n):
        stores.append(pltpu.make_async_copy(source, place, out_sem.at[n]))
        stores[-1].start()

    barrier = pltpu.get_barrier_semaphore()

    def greet(k, c):
        near = (row, lax.rem(col + 2 * k, 16))
        pl.semaphore_signal(barrier, inc=1, device_id=near, device_id_type=MESH)
        pl.semaphore_signal(barrier, inc=1, device_id=(lax.rem(row + k, 8), col), device_id_type=MESH)
        return c

    pl.semaphore_signal(barrier, inc=1, device_id=partner, device_id_type=MESH)
    lax.fori_loop(1, 8, greet, 0)
    for h in range(2):
        S[h][SLOTS] = jnp.zeros((TILE, TILE), F32)
    make_table(coords, count[0, 0], TABLE)
    table_copy = pltpu.make_async_copy(TABLE, table, table_sem)
    table_copy.start()
    for load in own_loads:
        load.wait()
    pl.semaphore_wait(barrier, 15)

    def spread(h, source, prev, src, contract, first=0, last=SLOTS):
        def step(k, c):
            term = lax.dot_general(
                T[k], source[table[src, k]], (((contract,), (0,)), ((), ())), preferred_element_type=F32
            )
            S[h][k] = S[h][table[prev, k]] + term
            return c

        lax.fori_loop(first, last, step, 0, unroll=32)

    def core_exchange(h):
        for b in range(8):
            for t in range(OWN):
                CS[h][b * OWN + t] = S[h][table[LAST_F, (b * 2 + 1 - co) * OWN + t]].astype(BF16)
        sent.append(send(CS[h], CR[h], cx_s.at[h], cx_r.at[h], partner))

    def forward_term(h, i, p, t):
        b = p * 4 + i
        return S[h][table[LAST_F, (b * 2 + co) * OWN + t]] + CR[h][b * OWN + t].astype(F32)

    def keep_aggregated(h, t, value):
        AGG[h][t * TILE:(t + 1) * TILE, :] = value.astype(BF16)

    gf = [gather(row_ring, F[h], gf_s.at[h], gf_r.at[h], sent) for h in range(2)]
    rf = [
        reduce(col_ring, functools.partial(forward_term, h), functools.partial(keep_aggregated, h),
               AS[h], AR[h], rf_s.at[h], rf_r.at[h], sent)
        for h in range(2)
    ]
    def products(h, first, last):
        if first == 0 and h == 0:
            table_copy.wait()
            for load in loads:
                load.wait()
        spread(h, F[h], PREV_F, SRC_F, 1, first, last)

    def from_core(h):
        arrive(CR[h], cx_s.at[h], cx_r.at[h], partner)

    f0, f1 = functools.partial(run, gf[0], 1), functools.partial(run, gf[1], 1)
    r0, r1 = functools.partial(run, rf[0], 1), functools.partial(run, rf[1], 1)
    p0 = functools.partial(products, 0, 0, SLOTS)
    p1a, p1b = functools.partial(products, 1, 0, SLOTS // 2), functools.partial(products, 1, SLOTS // 2, SLOTS)
    c0, c1 = functools.partial(core_exchange, 0), functools.partial(core_exchange, 1)
    w0, w1 = functools.partial(from_core, 0), functools.partial(from_core, 1)
    for step in (
        f0, f1, f0, f1, f0, f0, f0, f1, f1, f0, p0, c0, f1, f1, p1a, w0, r0, p1b, c1, w1, r1, r0, r0, r1, r1, r0, r1, r0, r1,
    ):
        step()

    def own_tile(t, c):
        rows = pl.ds(pl.multiple_of(t * TILE, TILE), TILE)
        pre = jnp.dot(AGG0[rows, :], weight[:TILE, :], preferred_element_type=F32)
        pre = pre + jnp.dot(AGG1[rows, :], weight[TILE:, :], preferred_element_type=F32)
        sigma = jax.nn.sigmoid(pre)
        ACT[rows, :] = (pre * sigma).astype(BF16)
        grad = out_grad[rows, :].astype(F32) * (sigma * (1.0 + pre * (1.0 - sigma)))
        grad = grad.astype(BF16)
        PG[rows, :] = grad
        for h in range(2):
            back = lax.dot_general(
                grad, weight[h * TILE:(h + 1) * TILE, :], (((1,), (1,)), ((), ())), preferred_element_type=F32
            )
            G[h][col * OWN + t] = back.astype(BF16)
        return c

    lax.fori_loop(0, OWN, own_tile, 0, unroll=2)

    def to_partner(h):
        count = [0]

        def landed(place):
            what = G[h].at[pl.ds(col_ring.block(*place) * OWN, OWN)]
            n = count[0]
            count[0] += 1
            sent.append(send(what, what, co_s.at[h, n], co_r.at[h, n], partner))

        return landed

    def from_partner(h):
        r = col_ring
        places = [(r.i, r.p), (r.i, r.q), (r.down, r.p), (r.up, r.p), (r.far, r.p), (r.down, r.q), (r.up, r.q), (r.far, r.q)]
        for n, (i, p) in enumerate(places):
            arrive(G[h].at[pl.ds((p * 8 + i * 2 + 1 - co) * OWN, OWN)], co_s.at[h, n], co_r.at[h, n], partner)

    def backward_term(h, i, p, t):
        return S[h][table[LAST_B, (i * 2 + p) * OWN + t]]

    def keep_feature_grad(h, t, value):
        FG[t * TILE:(t + 1) * TILE, h * TILE:(h + 1) * TILE] = value.astype(BF16)

    gb = [gather(col_ring, G[h], gb_s.at[h], gb_r.at[h], sent, to_partner(h)) for h in range(2)]
    rb = [
        reduce(row_ring, functools.partial(backward_term, h), functools.partial(keep_feature_grad, h),
               BS[h], BR[h], rb_s.at[h], rb_r.at[h], sent)
        for h in range(2)
    ]

    chip = col // 2
    half = pl.ds(pl.multiple_of(co * 128, 128), 128)
    other = pl.ds(pl.multiple_of((1 - co) * 128, 128), 128)
    here = pl.ds(pl.multiple_of(co * 128 + chip * 16, 16), 16)

    def weight_term():
        for h in range(2):
            WT[h * TILE:(h + 1) * TILE, :] = lax.dot_general(
                AGG[h][...], PG[...], (((0,), (0,)), ((), ())), preferred_element_type=F32
            )
        sent.append(send(WT.at[other], WX, wx_s.at[0], wx_r.at[0], partner))

    def weight_send():
        arrive(WX, wx_s.at[0], wx_r.at[0], partner)
        for n in range(8):
            WS[n] = WT[pl.ds(pl.multiple_of(co * 128 + n * 16, 16), 16), :] + WX[n * 16:(n + 1) * 16, :]
        WA[chip] = WS[chip]

        def go(k, c):
            to = lax.rem(chip + k, 8)
            send(WS.at[to], WA.at[chip], wa_s.at[k], wa_r.at[k], (row, to * 2 + co))
            return c

        lax.fori_loop(1, 8, go, 0)

    def weight_row():
        def got(k, c):
            fro = lax.rem(chip + 8 - k, 8)
            arrive(WA.at[fro], wa_s.at[k], wa_r.at[k], (row, fro * 2 + co))
            return c

        lax.fori_loop(1, 8, got, 0)
        total = WA[0]
        for n in range(1, 8):
            total = total + WA[n]
        WP[...] = total
        WB[row] = total

        def go(k, c):
            to = lax.rem(row + k, 8)
            send(WP, WB.at[row], wb_s.at[k], wb_r.at[k], (to, col))
            return c

        lax.fori_loop(1, 8, go, 0)

    def weight_back():
        def got(k, c):
            fro = lax.rem(row + 8 - k, 8)
            arrive(WB.at[fro], wb_s.at[k], wb_r.at[k], (fro, col))
            return c

        lax.fori_loop(1, 8, got, 0)
        total = WB[0]
        for n in range(1, 8):
            total = total + WB[n]
        WC[here, :] = total * scaling

        def go(k, c):
            to = lax.rem(chip + k, 8)
            send(WC.at[here], WC.at[here], wc_s.at[k], wc_r.at[k], (row, to * 2 + co))
            return c

        lax.fori_loop(1, 8, go, 0)

    def weight_share():
        def got(k, c):
            fro = lax.rem(chip + 8 - k, 8)
            arrive(WC.at[pl.ds(co * 128 + fro * 16, 16)], wc_s.at[k], wc_r.at[k], (row, fro * 2 + co))
            return c

        lax.fori_loop(1, 8, got, 0)
        sent.append(send(WC.at[half], WC.at[half], wx_s.at[1], wx_r.at[1], partner))

    def weight_end():
        arrive(WC.at[other], wx_s.at[1], wx_r.at[1], partner)
        store(WC, weight_grad, 1)

    store(ACT, activated, 0)

    def back_products(h, first, last):
        spread(h, G[h], PREV_B, SRC_B, 0, first, last)

    g0, g1 = functools.partial(run, gb[0], 1), functools.partial(run, gb[1], 1)
    r0, r1 = functools.partial(run, rb[0], 1), functools.partial(run, rb[1], 1)
    q0, q1 = functools.partial(from_partner, 0), functools.partial(from_partner, 1)
    a0, b0 = functools.partial(back_products, 0, 0, SLOTS // 2), functools.partial(back_products, 0, SLOTS // 2, SLOTS)
    a1, b1 = functools.partial(back_products, 1, 0, SLOTS // 2), functools.partial(back_products, 1, SLOTS // 2, SLOTS)
    wt, ws, wr, wb, wh, we = weight_term, weight_send, weight_row, weight_back, weight_share, weight_end
    for step in (
        g0, g0, g1, g0, wt, g0, g1, ws, g0, g1, g0, g1, q0, a0, b0, r0, g1, g1, wr, q1, a1, b1,
        r0, r1, r0, r1, wb, r0, r1, r1, wh, we, r0, r1,
    ):
        step()
    store(FG, feature_grad, 2)
    for copy in stores:
        copy.wait()

    for copy in sent:
        copy.wait_send()

    def gone(k, c):
        for ss, rs in ((wa_s, wa_r), (wb_s, wb_r), (wc_s, wc_r)):
            pltpu.make_async_remote_copy(
                src_ref=WP, dst_ref=WP, send_sem=ss.at[k], recv_sem=rs.at[k], device_id=partner, device_id_type=MESH
            ).wait_send()
        return c

    lax.fori_loop(1, 8, gone, 0)


def copy_kernel(*refs):
    count = len(refs) // 2
    for n in range(count):
        refs[count + n][...] = refs[n][...]


def keep(*arrays):
    where = pl.BlockSpec(memory_space=pltpu.VMEM)
    return pl.pallas_call(
        copy_kernel,
        out_shape=tuple(jax.ShapeDtypeStruct(a.shape, a.dtype) for a in arrays),
        in_specs=[where] * len(arrays),
        out_specs=(where,) * len(arrays),
    )(*arrays)


def body(scaling, features, weight, tile_values, tile_coords, tile_counts, out_grad):
    rows, width = features.shape
    hbm = pl.BlockSpec(memory_space=pl.ANY)
    tile = (TILE, TILE)

    def twice(count, kind=BF16):
        return [pltpu.VMEM((count,) + tile, kind)] * 2

    dma = pltpu.SemaphoreType.DMA
    outs = pl.pallas_call(
        functools.partial(kernel, scaling),
        out_shape=(
            jax.ShapeDtypeStruct((rows, width), BF16),
            jax.ShapeDtypeStruct((width, width), F32),
            jax.ShapeDtypeStruct((rows, width), BF16),
        ),
        in_specs=[
            pl.BlockSpec(memory_space=pltpu.SMEM), pl.BlockSpec(memory_space=pltpu.VMEM), hbm, hbm, hbm, hbm,
        ],
        out_specs=(hbm, hbm, hbm),
        scratch_shapes=[
            pltpu.VMEM((SLOTS,) + tile, BF16),
            *twice(SLOTS + 1, F32), *twice(COL_TILES), *twice(32), *twice(32), *twice(R_TILES), *twice(R_TILES),
            *twice(ROW_TILES), *twice(R_TILES), *twice(R_TILES),
            pltpu.VMEM((rows, TILE), BF16), pltpu.VMEM((rows, TILE), BF16), pltpu.VMEM((rows, width), BF16),
            pltpu.VMEM((width, width), F32), pltpu.VMEM((width // 2, width), F32), pltpu.VMEM((8, 16, width), F32),
            pltpu.VMEM((8, 16, width), F32), pltpu.VMEM((16, width), F32), pltpu.VMEM((8, 16, width), F32),
            pltpu.VMEM((width, width), F32), pltpu.VMEM((width, width), BF16), pltpu.VMEM((rows, width), BF16),
            pltpu.VMEM((rows, width), BF16), pltpu.VMEM((rows, width), BF16),
            pltpu.VMEM((8, WIDE), jnp.int32), pltpu.SMEM((8, WIDE), jnp.int32), dma(()),
            dma((8,)), dma((3,)), dma((6,)), dma((2, 11)), dma((2, 11)), dma((2,)), dma((2,)), dma((2, 11)), dma((2, 11)),
            dma((2, 11)), dma((2, 11)), dma((2, 8)), dma((2, 8)), dma((2, 11)), dma((2, 11)),
            dma((2,)), dma((2,)), dma((8,)), dma((8,)), dma((8,)), dma((8,)), dma((8,)), dma((8,)),
        ],
        compiler_params=pltpu.CompilerParams(
            collective_id=0, has_side_effects=True, vmem_limit_bytes=62 << 20
        ),
    )(tile_counts, tile_coords[0, 0].T, features, weight, tile_values[0, 0], out_grad)
    return keep(*outs)


def solution(mesh):
    nodes = 512 * mesh.shape["row"] * mesh.shape["col"]
    return jax.shard_map(
        functools.partial(body, float(nodes) ** -0.5),
        mesh=mesh,
        in_specs=(
            P(("row", "col"), None), P(), P("row", "col", None, None, None), P("row", "col", None, None),
            P("row", "col"), P(("row", "col"), None),
        ),
        out_specs=(P(("row", "col"), None), P(), P(("row", "col"), None)),
        check_vma=False,
    )
```

```python
import functools

import jax
import jax.numpy as jnp
from jax import lax
from jax.experimental import pallas as pl
from jax.experimental.pallas import tpu as pltpu
from jax.sharding import PartitionSpec as P

MESH = pl.DeviceIdType.MESH
TILE = 128
SLOTS = 192
ROW_TILES = 64
COL_TILES = 32
OWN = 4
HALF = 2
WIDE = 256
PREV_F, SRC_F, LAST_F, PREV_B, SRC_B, LAST_B = range(6)
R_FARP, R_NEARP_U, R_NEARP_D, R_FAR_U, R_FAR_D, R_NEAR_U, R_NEAR_D, R_PAIR = 0, 4, 8, 12, 14, 16, 20, 24
R_TILES = 28
F32 = jnp.float32
BF16 = jnp.bfloat16


def send(src, dst, ssem, rsem, device):
    copy = pltpu.make_async_remote_copy(
        src_ref=src, dst_ref=dst, send_sem=ssem, recv_sem=rsem, device_id=device, device_id_type=MESH
    )
    copy.start()
    return copy


def arrive(dst, ssem, rsem, device):
    pltpu.make_async_remote_copy(
        src_ref=dst, dst_ref=dst, send_sem=ssem, recv_sem=rsem, device_id=device, device_id_type=MESH
    ).wait_recv()


def run(steps, count):
    for _ in range(count):
        next(steps)


class Ring:
    def __init__(self, i, p, device, block):
        self.up, self.down, self.far = lax.rem(i + 1, 4), lax.rem(i + 3, 4), lax.rem(i + 2, 4)
        self.i, self.p, self.q = i, p, 1 - p
        self.d_up, self.d_down, self.d_pair = device(self.up, p), device(self.down, p), device(i, self.q)
        self.block = block


def gather(ring, buf, ss, rs, sent, landed=lambda name: None):
    i, p, q, up, down, far = ring.i, ring.p, ring.q, ring.up, ring.down, ring.far

    def part(i, p, first=0, count=OWN):
        return buf.at[pl.ds(ring.block(i, p) * OWN + first, count)]

    def go(n, what, device):
        sent.append(send(what, what, ss.at[n], rs.at[n], device))

    def got(n, what, device):
        arrive(what, ss.at[n], rs.at[n], device)

    go(0, part(i, p, 0, HALF), ring.d_up)
    go(1, part(i, p, HALF, HALF), ring.d_down)
    go(4, part(i, p), ring.d_pair)
    go(2, part(i, p, HALF, HALF), ring.d_up)
    go(3, part(i, p, 0, HALF), ring.d_down)
    landed((i, p))
    yield
    got(0, part(down, p, 0, HALF), ring.d_down)
    go(5, part(down, p, 0, HALF), ring.d_up)
    got(1, part(up, p, HALF, HALF), ring.d_up)
    go(6, part(up, p, HALF, HALF), ring.d_down)
    yield
    got(4, part(i, q), ring.d_pair)
    go(7, part(i, q), ring.d_up)
    go(8, part(i, q), ring.d_down)
    landed((i, q))
    got(2, part(down, p, HALF, HALF), ring.d_down)
    landed((down, p))
    got(3, part(up, p, 0, HALF), ring.d_up)
    landed((up, p))
    yield
    got(5, part(far, p, 0, HALF), ring.d_down)
    go(9, part(far, p, 0, HALF), ring.d_pair)
    got(6, part(far, p, HALF, HALF), ring.d_up)
    go(10, part(far, p, HALF, HALF), ring.d_pair)
    landed((far, p))
    yield
    got(7, part(down, q), ring.d_down)
    landed((down, q))
    got(8, part(up, q), ring.d_up)
    landed((up, q))
    yield
    got(9, part(far, q, 0, HALF), ring.d_pair)
    got(10, part(far, q, HALF, HALF), ring.d_pair)
    landed((far, q))
    yield


def reduce(ring, partial, out, sbuf, rbuf, ss, rs, sent, ready=lambda: None):
    i, p, q, up, down, far = ring.i, ring.p, ring.q, ring.up, ring.down, ring.far

    def go(n, first, count, device):
        sent.append(
            send(sbuf.at[pl.ds(first, count)], rbuf.at[pl.ds(first, count)], ss.at[n], rs.at[n], device)
        )

    def got(n, first, count, device):
        arrive(rbuf.at[pl.ds(first, count)], ss.at[n], rs.at[n], device)

    def put(first, block, tiles=range(OWN), terms=()):
        for n, t in enumerate(tiles):
            total = partial(*block, t)
            for term in terms:
                total = total + rbuf[term + n].astype(F32)
            sbuf[first + n] = total.astype(BF16)

    put(R_FARP, (far, q))
    go(0, R_FARP, HALF, ring.d_pair)
    go(1, R_FARP + HALF, HALF, ring.d_pair)
    put(R_NEARP_U, (up, q))
    go(2, R_NEARP_U, OWN, ring.d_up)
    put(R_NEARP_D, (down, q))
    go(3, R_NEARP_D, OWN, ring.d_down)
    ready()
    put(R_NEAR_U + HALF, (up, p), (2, 3))
    go(4, R_NEAR_U + HALF, HALF, ring.d_up)
    put(R_NEAR_D, (down, p), (0, 1))
    go(5, R_NEAR_D, HALF, ring.d_down)
    yield
    got(0, R_FARP, HALF, ring.d_pair)
    put(R_FAR_U, (far, p), (0, 1), (R_FARP,))
    go(6, R_FAR_U, HALF, ring.d_up)
    got(1, R_FARP + HALF, HALF, ring.d_pair)
    put(R_FAR_D, (far, p), (2, 3), (R_FARP + HALF,))
    go(7, R_FAR_D, HALF, ring.d_down)
    yield
    got(2, R_NEARP_U, OWN, ring.d_down)
    got(3, R_NEARP_D, OWN, ring.d_up)
    put(R_PAIR, (i, q), range(OWN), (R_NEARP_U, R_NEARP_D))
    go(8, R_PAIR, OWN, ring.d_pair)
    yield
    got(6, R_FAR_U, HALF, ring.d_down)
    put(R_NEAR_U, (up, p), (0, 1), (R_FAR_U,))
    go(9, R_NEAR_U, HALF, ring.d_up)
    got(7, R_FAR_D, HALF, ring.d_up)
    put(R_NEAR_D + HALF, (down, p), (2, 3), (R_FAR_D,))
    go(10, R_NEAR_D + HALF, HALF, ring.d_down)
    yield
    got(4, R_NEAR_U + HALF, HALF, ring.d_down)
    got(5, R_NEAR_D, HALF, ring.d_up)
    got(8, R_PAIR, OWN, ring.d_pair)
    got(9, R_NEAR_U, HALF, ring.d_down)
    got(10, R_NEAR_D + HALF, HALF, ring.d_up)
    for t in range(OWN):
        total = partial(i, p, t)
        for term in (R_PAIR, R_NEAR_U, R_NEAR_D):
            total = total + rbuf[term + t].astype(F32)
        out(t, total)
    yield


def make_table(coords, count, out):
    first = lax.broadcasted_iota(jnp.int32, (WIDE, WIDE), 0)
    second = lax.broadcasted_iota(jnp.int32, (WIDE, WIDE), 1)
    out[...] = jnp.zeros_like(out)
    pad = jnp.zeros((1, WIDE - SLOTS), jnp.int32)
    lane = lax.broadcasted_iota(jnp.int32, (1, WIDE), 1)
    for group, source, rows in ((0, 1, (PREV_F, SRC_F, LAST_F)), (1, 0, (PREV_B, SRC_B, LAST_B))):
        place = jnp.concatenate([coords[group:group + 1, :], pad], axis=1)
        taken = jnp.concatenate([coords[source:source + 1, :], pad], axis=1)
        along = jnp.broadcast_to(place, (WIDE, WIDE))
        across = along.T
        before = jnp.where((across == along) & (first < second) & (first < count), first, -1)
        previous = jnp.max(before, axis=0, keepdims=True)
        inside = jnp.where((across == second) & (first < count), first, -1)
        last = jnp.max(inside, axis=0, keepdims=True)
        out[rows[0]:rows[0] + 1, :] = jnp.where(previous < 0, SLOTS, previous)
        out[rows[1]:rows[1] + 1, :] = jnp.where(lane < count, taken, 0)
        out[rows[2]:rows[2] + 1, :] = jnp.where(last < 0, SLOTS, last)


def kernel(
    scaling, count, coords, features, weight_hbm, tiles, out_grad_hbm, activated, weight_grad, feature_grad,
    T, S0, S1, F0, F1, CS0, CS1, CR0, CR1, AS0, AS1, AR0, AR1, G0, G1, BS0, BS1, BR0, BR1,
    AGG0, AGG1, PG, WT, WX, WS, WA, WP, WB, WC, weight, out_grad, ACT, FG,
    TABLE, table, table_sem, own_sem, out_sem, tile_sem, gf_s, gf_r, cx_s, cx_r, rf_s, rf_r, gb_s, gb_r, co_s, co_r, rb_s, rb_r,
    wx_s, wx_r, wa_s, wa_r, wb_s, wb_r, wc_s, wc_r,
):
    S, F, CS, CR, AS, AR = (S0, S1), (F0, F1), (CS0, CS1), (CR0, CR1), (AS0, AS1), (AR0, AR1)
    G, BS, BR, AGG = (G0, G1), (BS0, BS1), (BR0, BR1), (AGG0, AGG1)
    row, col = lax.axis_index("row"), lax.axis_index("col")
    x, zl = row // 2, lax.rem(row, 2)
    zh, y, co = col // 8, lax.rem(col, 8) // 2, lax.rem(col, 2)
    row_ring = Ring(x, zl, lambda i, p: (i * 2 + p, col), lambda i, p: i * 2 + p)
    col_ring = Ring(y, zh, lambda i, p: (row, p * 8 + i * 2 + co), lambda i, p: p * 8 + i * 2 + co)
    partner = (row, zh * 8 + y * 2 + 1 - co)
    sent = []

    own_loads = []
    for h in range(2):
        for t in range(OWN):
            own_loads.append(
                pltpu.make_async_copy(
                    features.at[pl.ds(t * TILE, TILE), pl.ds(h * TILE, TILE)], F[h].at[row * OWN + t],
                    own_sem.at[h * OWN + t],
                )
            )
            own_loads[-1].start()
    loads = []
    for n in range(4):
        span = pl.ds(n * (SLOTS // 4), SLOTS // 4)
        loads.append(pltpu.make_async_copy(tiles.at[span], T.at[span], tile_sem.at[n]))
        loads[-1].start()

    for source, place in ((weight_hbm, weight), (out_grad_hbm, out_grad)):
        loads.append(pltpu.make_async_copy(source, place, tile_sem.at[len(loads)]))
        loads[-1].start()
    stores = []

    def store(source, place, n):
        stores.append(pltpu.make_async_copy(source, place, out_sem.at[n]))
        stores[-1].start()

    barrier = pltpu.get_barrier_semaphore()

    def greet(k, c):
        near = (row, lax.rem(col + 2 * k, 16))
        pl.semaphore_signal(barrier, inc=1, device_id=near, device_id_type=MESH)
        pl.semaphore_signal(barrier, inc=1, device_id=(lax.rem(row + k, 8), col), device_id_type=MESH)
        return c

    pl.semaphore_signal(barrier, inc=1, device_id=partner, device_id_type=MESH)
    lax.fori_loop(1, 8, greet, 0)
    for h in range(2):
        S[h][SLOTS] = jnp.zeros((TILE, TILE), F32)
    make_table(coords, count[0, 0], TABLE)
    table_copy = pltpu.make_async_copy(TABLE, table, table_sem)
    table_copy.start()
    for load in own_loads:
        load.wait()
    pl.semaphore_wait(barrier, 15)

    def spread(h, source, prev, src, contract, first=0, last=SLOTS):
        def step(k, c):
            term = lax.dot_general(
                T[k], source[table[src, k]], (((contract,), (0,)), ((), ())), preferred_element_type=F32
            )
            S[h][k] = S[h][table[prev, k]] + term
            return c

        lax.fori_loop(first, last, step, 0, unroll=48)

    def core_exchange(h):
        for n, p in enumerate((1 - zh, zh)):
            for b in range(4):
                for t in range(OWN):
                    place = p * 4 + b
                    CS[h][place * OWN + t] = S[h][table[LAST_F, (place * 2 + 1 - co) * OWN + t]].astype(BF16)
            span = pl.ds(p * 16, 16)
            sent.append(send(CS[h].at[span], CR[h].at[span], cx_s.at[h, n], cx_r.at[h, n], partner))

    def forward_term(h, i, p, t):
        b = p * 4 + i
        return S[h][table[LAST_F, (b * 2 + co) * OWN + t]] + CR[h][b * OWN + t].astype(F32)

    def keep_aggregated(h, t, value):
        AGG[h][t * TILE:(t + 1) * TILE, :] = value.astype(BF16)

    def from_core(h):
        arrive(CR[h].at[pl.ds((1 - zh) * 16, 16)], cx_s.at[h, 0], cx_r.at[h, 0], partner)

    def from_core_rest(h):
        arrive(CR[h].at[pl.ds(zh * 16, 16)], cx_s.at[h, 1], cx_r.at[h, 1], partner)

    gf = [gather(row_ring, F[h], gf_s.at[h], gf_r.at[h], sent) for h in range(2)]
    rf = [
        reduce(col_ring, functools.partial(forward_term, h), functools.partial(keep_aggregated, h),
               AS[h], AR[h], rf_s.at[h], rf_r.at[h], sent, functools.partial(from_core_rest, h))
        for h in range(2)
    ]
    def products(h, first, last):
        if first == 0 and h == 0:
            table_copy.wait()
            for load in loads:
                load.wait()
        spread(h, F[h], PREV_F, SRC_F, 1, first, last)

    f0, f1 = functools.partial(run, gf[0], 1), functools.partial(run, gf[1], 1)
    r0, r1 = functools.partial(run, rf[0], 1), functools.partial(run, rf[1], 1)
    p0 = functools.partial(products, 0, 0, SLOTS)
    p1a, p1b = functools.partial(products, 1, 0, SLOTS // 2), functools.partial(products, 1, SLOTS // 2, SLOTS)
    c0, c1 = functools.partial(core_exchange, 0), functools.partial(core_exchange, 1)
    w0, w1 = functools.partial(from_core, 0), functools.partial(from_core, 1)
    for step in (
        f0, f1, f0, f1, f0, f0, f0, f1, f1, f0, p0, c0, f1, f1, p1a, w0, r0, p1b, c1, w1, r1, r0, r0, r1, r1, r0, r1, r0, r1,
    ):
        step()

    def own_tile(t, c):
        rows = pl.ds(pl.multiple_of(t * TILE, TILE), TILE)
        pre = jnp.dot(AGG0[rows, :], weight[:TILE, :], preferred_element_type=F32)
        pre = pre + jnp.dot(AGG1[rows, :], weight[TILE:, :], preferred_element_type=F32)
        sigma = jax.nn.sigmoid(pre)
        ACT[rows, :] = (pre * sigma).astype(BF16)
        grad = out_grad[rows, :].astype(F32) * (sigma * (1.0 + pre * (1.0 - sigma)))
        grad = grad.astype(BF16)
        PG[rows, :] = grad
        for h in range(2):
            back = lax.dot_general(
                grad, weight[h * TILE:(h + 1) * TILE, :], (((1,), (1,)), ((), ())), preferred_element_type=F32
            )
            G[h][col * OWN + t] = back.astype(BF16)
        return c

    lax.fori_loop(0, OWN, own_tile, 0, unroll=2)

    def to_partner(h):
        count = [0]

        def landed(place):
            what = G[h].at[pl.ds(col_ring.block(*place) * OWN, OWN)]
            n = count[0]
            count[0] += 1
            sent.append(send(what, what, co_s.at[h, n], co_r.at[h, n], partner))

        return landed

    def from_partner(h):
        r = col_ring
        places = [(r.i, r.p), (r.i, r.q), (r.down, r.p), (r.up, r.p), (r.far, r.p), (r.down, r.q), (r.up, r.q), (r.far, r.q)]
        for n, (i, p) in enumerate(places):
            arrive(G[h].at[pl.ds((p * 8 + i * 2 + 1 - co) * OWN, OWN)], co_s.at[h, n], co_r.at[h, n], partner)

    def backward_term(h, i, p, t):
        return S[h][table[LAST_B, (i * 2 + p) * OWN + t]]

    def keep_feature_grad(h, t, value):
        FG[t * TILE:(t + 1) * TILE, h * TILE:(h + 1) * TILE] = value.astype(BF16)

    gb = [gather(col_ring, G[h], gb_s.at[h], gb_r.at[h], sent, to_partner(h)) for h in range(2)]
    rb = [
        reduce(row_ring, functools.partial(backward_term, h), functools.partial(keep_feature_grad, h),
               BS[h], BR[h], rb_s.at[h], rb_r.at[h], sent)
        for h in range(2)
    ]

    chip = col // 2
    half = pl.ds(pl.multiple_of(co * 128, 128), 128)
    other = pl.ds(pl.multiple_of((1 - co) * 128, 128), 128)
    here = pl.ds(pl.multiple_of(co * 128 + chip * 16, 16), 16)

    def weight_term():
        for h in range(2):
            WT[h * TILE:(h + 1) * TILE, :] = lax.dot_general(
                AGG[h][...], PG[...], (((0,), (0,)), ((), ())), preferred_element_type=F32
            )
        sent.append(send(WT.at[other], WX, wx_s.at[0], wx_r.at[0], partner))

    def weight_send():
        arrive(WX, wx_s.at[0], wx_r.at[0], partner)
        for n in range(8):
            WS[n] = WT[pl.ds(pl.multiple_of(co * 128 + n * 16, 16), 16), :] + WX[n * 16:(n + 1) * 16, :]
        WA[chip] = WS[chip]

        def go(k, c):
            to = lax.rem(chip + k, 8)
            send(WS.at[to], WA.at[chip], wa_s.at[k], wa_r.at[k], (row, to * 2 + co))
            return c

        lax.fori_loop(1, 8, go, 0)

    def weight_row():
        def got(k, c):
            fro = lax.rem(chip + 8 - k, 8)
            arrive(WA.at[fro], wa_s.at[k], wa_r.at[k], (row, fro * 2 + co))
            return c

        lax.fori_loop(1, 8, got, 0)
        total = WA[0]
        for n in range(1, 8):
            total = total + WA[n]
        WP[...] = total
        WB[row] = total

        def go(k, c):
            to = lax.rem(row + k, 8)
            send(WP, WB.at[row], wb_s.at[k], wb_r.at[k], (to, col))
            return c

        lax.fori_loop(1, 8, go, 0)

    def weight_back():
        def got(k, c):
            fro = lax.rem(row + 8 - k, 8)
            arrive(WB.at[fro], wb_s.at[k], wb_r.at[k], (fro, col))
            return c

        lax.fori_loop(1, 8, got, 0)
        total = WB[0]
        for n in range(1, 8):
            total = total + WB[n]
        WC[here, :] = total * scaling

        def go(k, c):
            to = lax.rem(chip + k, 8)
            send(WC.at[here], WC.at[here], wc_s.at[k], wc_r.at[k], (row, to * 2 + co))
            return c

        lax.fori_loop(1, 8, go, 0)

    def weight_share():
        def got(k, c):
            fro = lax.rem(chip + 8 - k, 8)
            arrive(WC.at[pl.ds(co * 128 + fro * 16, 16)], wc_s.at[k], wc_r.at[k], (row, fro * 2 + co))
            return c

        lax.fori_loop(1, 8, got, 0)
        sent.append(send(WC.at[half], WC.at[half], wx_s.at[1], wx_r.at[1], partner))

    def weight_end():
        arrive(WC.at[other], wx_s.at[1], wx_r.at[1], partner)
        store(WC, weight_grad, 1)

    store(ACT, activated, 0)

    def back_products(h, first, last):
        spread(h, G[h], PREV_B, SRC_B, 0, first, last)

    g0, g1 = functools.partial(run, gb[0], 1), functools.partial(run, gb[1], 1)
    r0, r1 = functools.partial(run, rb[0], 1), functools.partial(run, rb[1], 1)
    q0, q1 = functools.partial(from_partner, 0), functools.partial(from_partner, 1)
    a0, b0 = functools.partial(back_products, 0, 0, SLOTS // 2), functools.partial(back_products, 0, SLOTS // 2, SLOTS)
    a1, b1 = functools.partial(back_products, 1, 0, SLOTS // 2), functools.partial(back_products, 1, SLOTS // 2, SLOTS)
    wt, ws, wr, wb, wh, we = weight_term, weight_send, weight_row, weight_back, weight_share, weight_end
    for step in (
        g0, g0, g1, g0, wt, g0, g1, ws, g0, g1, g0, g1, q0, a0, b0, r0, g1, g1, wr, q1, a1, b1,
        r0, r1, r0, r1, wb, r0, r1, r1, wh, we, r0, r1,
    ):
        step()
    store(FG, feature_grad, 2)
    for copy in stores:
        copy.wait()

    for copy in sent:
        copy.wait_send()

    def gone(k, c):
        for ss, rs in ((wa_s, wa_r), (wb_s, wb_r), (wc_s, wc_r)):
            pltpu.make_async_remote_copy(
                src_ref=WP, dst_ref=WP, send_sem=ss.at[k], recv_sem=rs.at[k], device_id=partner, device_id_type=MESH
            ).wait_send()
        return c

    lax.fori_loop(1, 8, gone, 0)


def copy_kernel(*refs):
    count = len(refs) // 2
    for n in range(count):
        refs[count + n][...] = refs[n][...]


def keep(*arrays):
    where = pl.BlockSpec(memory_space=pltpu.VMEM)
    return pl.pallas_call(
        copy_kernel,
        out_shape=tuple(jax.ShapeDtypeStruct(a.shape, a.dtype) for a in arrays),
        in_specs=[where] * len(arrays),
        out_specs=(where,) * len(arrays),
    )(*arrays)


def body(scaling, features, weight, tile_values, tile_coords, tile_counts, out_grad):
    rows, width = features.shape
    hbm = pl.BlockSpec(memory_space=pl.ANY)
    tile = (TILE, TILE)

    def twice(count, kind=BF16):
        return [pltpu.VMEM((count,) + tile, kind)] * 2

    dma = pltpu.SemaphoreType.DMA
    outs = pl.pallas_call(
        functools.partial(kernel, scaling),
        out_shape=(
            jax.ShapeDtypeStruct((rows, width), BF16),
            jax.ShapeDtypeStruct((width, width), F32),
            jax.ShapeDtypeStruct((rows, width), BF16),
        ),
        in_specs=[
            pl.BlockSpec(memory_space=pltpu.SMEM), pl.BlockSpec(memory_space=pltpu.VMEM), hbm, hbm, hbm, hbm,
        ],
        out_specs=(hbm, hbm, hbm),
        scratch_shapes=[
            pltpu.VMEM((SLOTS,) + tile, BF16),
            *twice(SLOTS + 1, F32), *twice(COL_TILES), *twice(32), *twice(32), *twice(R_TILES), *twice(R_TILES),
            *twice(ROW_TILES), *twice(R_TILES), *twice(R_TILES),
            pltpu.VMEM((rows, TILE), BF16), pltpu.VMEM((rows, TILE), BF16), pltpu.VMEM((rows, width), BF16),
            pltpu.VMEM((width, width), F32), pltpu.VMEM((width // 2, width), F32), pltpu.VMEM((8, 16, width), F32),
            pltpu.VMEM((8, 16, width), F32), pltpu.VMEM((16, width), F32), pltpu.VMEM((8, 16, width), F32),
            pltpu.VMEM((width, width), F32), pltpu.VMEM((width, width), BF16), pltpu.VMEM((rows, width), BF16),
            pltpu.VMEM((rows, width), BF16), pltpu.VMEM((rows, width), BF16),
            pltpu.VMEM((8, WIDE), jnp.int32), pltpu.SMEM((8, WIDE), jnp.int32), dma(()),
            dma((8,)), dma((3,)), dma((6,)), dma((2, 11)), dma((2, 11)), dma((2, 2)), dma((2, 2)), dma((2, 11)), dma((2, 11)),
            dma((2, 11)), dma((2, 11)), dma((2, 8)), dma((2, 8)), dma((2, 11)), dma((2, 11)),
            dma((2,)), dma((2,)), dma((8,)), dma((8,)), dma((8,)), dma((8,)), dma((8,)), dma((8,)),
        ],
        compiler_params=pltpu.CompilerParams(
            collective_id=0, has_side_effects=True, vmem_limit_bytes=62 << 20
        ),
    )(tile_counts, tile_coords[0, 0].T, features, weight, tile_values[0, 0], out_grad)
    return keep(*outs)


def solution(mesh):
    nodes = 512 * mesh.shape["row"] * mesh.shape["col"]
    return jax.shard_map(
        functools.partial(body, float(nodes) ** -0.5),
        mesh=mesh,
        in_specs=(
            P(("row", "col"), None), P(), P("row", "col", None, None, None), P("row", "col", None, None),
            P("row", "col"), P(("row", "col"), None),
        ),
        out_specs=(P(("row", "col"), None), P(), P(("row", "col"), None)),
        check_vma=False,
    )
```
